256 devices in a mesh: normal: 2 (over x_lo), surf: 128 (over z, y, x_hi, core).
Axes of the slice: x: 4 (x_hi: 2, x_lo: 2; x = x_hi * 2 + x_lo), y: 4, z: 8, core: 2. Of those that a mesh axis runs over, the one named last changes fastest.
Arguments:
- populations: bfloat16 [256, 32, 16384], P(None, 'normal', 'surf'), may hold values from 0.1 to 60, as said below
- absorb_table: bfloat16 [128, 256], replicated, may hold values from 2.9e-06 to 0.0031, as said below
- emit_table: bfloat16 [128, 256], replicated, may hold values from 2.9e-06 to 0.0031, as said below
- energy: float32 [128, 32, 16384], P(None, 'normal', 'surf'), may hold values from 0.2 to 1.5
- wall_source: float32 [128], replicated, may hold values from 0.5 to 2
- neighbours: int32 [16384, 4], P('surf'), may hold values from -1 to 16383, as said below
- wall_type: int32 [16384], P('surf'), may hold values from 0 to 2
Outputs:
- energy_out: float32 [128, 32, 16384], P(None, 'normal', 'surf')
The draws below stay inside these ranges and needn't reach their ends.
Inputs may be any that keep to these rules, and one draw needn't show every extreme that they name: `neighbours`: every entry that is not -1 is another surface cell within 32 positions of the cell itself; some entry lies exactly 32 away. `populations`: populations are positive. `absorb_table`: entries are positive. `emit_table`: entries are positive.
All inputs are finite; a program needn't handle non-finite values.
Results may differ from the reference program's by a relative error of at most 0.0003.
Values sent between devices are 32-bit elements; how exact they have to be, the bound alone decides.
No kernel may reach another device: no remote copies, remote signals or barrier semaphores. Data moves between devices by JAX's collectives and lax.ppermute only.
A program may use at most 64 MiB of HBM per device.

```python
import math
import jax
import jax.numpy as jnp
from jax import lax

GROUPS = 128
LEVELS = 256
ITERS = 2
HALO = 32
NN = 32
SURFACE = 16384


def sparse_table(key):
    base_key, mask_key, large_key = jax.random.split(key, 3)
    base = jnp.exp(jax.random.uniform(base_key, (GROUPS, LEVELS), jnp.float32, jnp.log(3e-06), jnp.log(3e-05)))
    large = jnp.exp(jax.random.uniform(large_key, (GROUPS, LEVELS), jnp.float32, jnp.log(0.0003), jnp.log(0.003)))
    chosen = jax.random.randint(mask_key, (GROUPS, LEVELS), 0, 16) == 0
    return jnp.where(chosen, large, base).astype(jnp.bfloat16)


def draw_absorb_table(key, part):
    key = jax.random.fold_in(key, 31)
    return sparse_table(key)


def draw_emit_table(key, part):
    key = jax.random.fold_in(key, 37)
    return sparse_table(key)


def draw_populations(key, part):
    cell_key, level_key = jax.random.split(jax.random.fold_in(key, 11))
    cell_scale = jnp.exp(jax.random.uniform(cell_key, (1, NN, SURFACE), jnp.float32, 0.0, 4.0))
    level_scale = jnp.exp(jax.random.uniform(level_key, (LEVELS, NN, SURFACE), jnp.float32, -2.3, 2.3))
    return jnp.clip(cell_scale * level_scale, 0.1, 60.0).astype(jnp.bfloat16)


def draw_neighbours(key, part):
    order_key, sign_key, extra_key, drop_key = jax.random.split(jax.random.fold_in(key, 23), 4)
    cells = jnp.arange(SURFACE, dtype=jnp.int32)
    first_reach = 1 + jax.random.permutation(order_key, SURFACE).astype(jnp.int32) % HALO
    other_reach = jax.random.randint(extra_key, (SURFACE, 3), 1, HALO + 1).astype(jnp.int32)
    reach = jnp.concatenate([first_reach[:, None], other_reach], axis=1)
    signs = 2 * jax.random.randint(sign_key, (SURFACE, 4), 0, 2).astype(jnp.int32) - 1
    target = cells[:, None] + signs * reach
    dropped = jax.random.randint(drop_key, (SURFACE, 4), 0, 8) == 0
    inside = (target >= 0) & (target < SURFACE) & jnp.logical_not(dropped)
    return jnp.where(inside, target, -1).astype(jnp.int32)


def set_ends(values, key, smallest, largest):
    index_at = [jax.random.randint(jax.random.fold_in(key, axis), (), 0, length) for axis, length in enumerate(values.shape)]
    main_axis = values.shape.index(max(values.shape))
    beside = index_at[:main_axis] + [(index_at[main_axis] + 1) % values.shape[main_axis]] + index_at[main_axis + 1:]
    return values.at[tuple(index_at)].set(smallest).at[tuple(beside)].set(largest)


def block_scale(stream_key, dims, shards, low, high):
    gain, own = 1.0, jax.random.fold_in(stream_key, 6)
    for axis_at, shards_of in shards:
        steps = jnp.exp(jax.random.uniform(jax.random.fold_in(own, axis_at), (shards_of,), jnp.float32, low / len(shards), high / len(shards)))
        gain = gain * jnp.repeat(steps, dims[axis_at] // shards_of).reshape([-1 if axis == axis_at else 1 for axis in range(len(dims))])
    return gain


def setup_inputs(seed: int = 0) -> dict:
    key_list = jax.random.split(jax.random.key(seed), 8)
    populations = draw_populations(jax.random.fold_in(key_list[7], 71), 0)
    absorb_table = draw_absorb_table(jax.random.fold_in(key_list[7], 71), 0)
    emit_table = draw_emit_table(jax.random.fold_in(key_list[7], 71), 0)
    energy = jnp.clip(0.2 + 1.3 * jax.random.uniform(key_list[3], (GROUPS, NN, SURFACE), jnp.float32) ** block_scale(key_list[3], (GROUPS, NN, SURFACE), ((1, 2), (2, 128)), -0.2, 0.2), 0.2, 1.5)
    wall_source = jnp.clip(jnp.exp(jax.random.uniform(key_list[4], (GROUPS,), jnp.float32, math.log(0.5), math.log(2.0))), 0.5, 2.0)
    neighbours = draw_neighbours(jax.random.fold_in(key_list[7], 71), 0)
    wall_type = set_ends(jax.random.randint(key_list[6], (SURFACE,), 0, 3), jax.random.fold_in(key_list[6], 1), 0, 2).astype(jnp.int32)
    return {"populations": populations, "absorb_table": absorb_table, "emit_table": emit_table, "energy": energy, "wall_source": wall_source, "neighbours": neighbours, "wall_type": wall_type}


SURF_WEIGHT = 0.02


def face_value(left, right):
    return 2.0 / (3.0 * (left + right))


def tridiagonal(lower, diag, upper, rhs):
    lined = tuple(jnp.moveaxis(value, 1, 0) for value in (lower, diag, upper, rhs))
    zero_row = jnp.zeros(lined[0].shape[1:], jnp.float32)

    def forward(carry, line_row):
        carried, solved = carry
        low_coef, diag_coef, up_coef, rhs_coef = line_row
        denominator = diag_coef - low_coef * carried
        new_carried = up_coef / denominator
        new_solved = (rhs_coef - low_coef * solved) / denominator
        return (new_carried, new_solved), (new_carried, new_solved)

    unused, (all_carried, all_solved) = lax.scan(forward, (zero_row, zero_row), lined)

    def backward(after, line_row):
        carried, solved = line_row
        value = solved - carried * after
        return value, value

    unused_last, values = lax.scan(backward, zero_row, (all_carried, all_solved), reverse=True)
    return jnp.moveaxis(values, 0, 1)


def reference(populations, absorb_table, emit_table, energy, wall_source, neighbours, wall_type):
    flat = populations.reshape(LEVELS, NN * SURFACE)
    valid = neighbours >= 0
    places = jnp.where(valid, neighbours, 0).astype(jnp.int32)
    wall_weight = jnp.where(wall_type == 0, 0.5, jnp.where(wall_type == 1, 0.25, 0.0)).astype(jnp.float32)
    row_ids = lax.broadcasted_iota(jnp.int32, (1, NN, 1), 1)
    wall_row = row_ids == 0
    outer_row = row_ids == NN - 1
    blocks = GROUPS // 8

    def one_block(block_items):
        absorb, emit, start, source = block_items
        kappa = jnp.dot(absorb, flat, preferred_element_type=jnp.float32).reshape(8, NN, SURFACE)
        emission = jnp.dot(emit, flat, preferred_element_type=jnp.float32).reshape(8, NN, SURFACE)
        faces = face_value(kappa[:, :-1, :], kappa[:, 1:, :])
        zero_face = jnp.zeros((8, 1, SURFACE), jnp.float32)
        lower = jnp.concatenate([zero_face, -faces], axis=1)
        upper = jnp.concatenate([-faces, zero_face], axis=1)
        couples = [jnp.where(valid[:, slot], SURF_WEIGHT * face_value(kappa, kappa[:, :, places[:, slot]]), 0.0) for slot in range(4)]
        boundary = jnp.where(wall_row, wall_weight[None, None, :], 0.0) + jnp.where(outer_row, 0.5, 0.0)
        diag = kappa - lower - upper + (couples[0] + couples[1] + couples[2] + couples[3]) + boundary
        wall_rhs = jnp.where(wall_row, wall_weight[None, None, :] * source[:, None, None], 0.0)
        current = start
        for step in range(ITERS):
            gathered = couples[0] * current[:, :, places[:, 0]] + couples[1] * current[:, :, places[:, 1]] + couples[2] * current[:, :, places[:, 2]] + couples[3] * current[:, :, places[:, 3]]
            rhs = emission + gathered + wall_rhs
            current = tridiagonal(lower, diag, upper, rhs)
        return current

    result = lax.map(one_block, (absorb_table.reshape(blocks, 8, LEVELS), emit_table.reshape(blocks, 8, LEVELS), energy.reshape(blocks, 8, NN, SURFACE), wall_source.reshape(blocks, 8)))
    return result.reshape(GROUPS, NN, SURFACE)
```

```python
import jax
import jax.numpy as jnp
from jax import lax
from jax.experimental import pallas as pl
from jax.experimental.pallas import tpu as pltpu
from jax.sharding import PartitionSpec as P

HALO = 32
LANES = 128
SURF_WEIGHT = 0.02
FACE = 2.0 / 3.0
LIMIT = 32 * 1024 * 1024


def inverse(value):
    guess = pl.reciprocal(value, approx=True)
    return guess * (2.0 - value * guess)


def lane_ids(rows):
    return lax.broadcasted_iota(jnp.int32, (rows, LANES), 1)


def gather(value, lanes):
    return jnp.take_along_axis(value, lanes, axis=1, mode="promise_in_bounds")


def row_of(position, count):
    block = lax.axis_index("normal")
    return position + block * (count - 1 - 2 * position)


def pack_sides(planes, forward_ref, backward_ref, lead):
    groups = planes[0].shape[0]
    slot = lane_ids(groups) // HALO
    for part in range(len(planes) // 4):
        four = planes[4 * part : 4 * part + 4]
        ahead, back = [], []
        for k in range(4):
            turn = (HALO * (k + 1)) % LANES
            ahead.append(pltpu.roll(four[k], turn, 1) if turn else four[k])
            turn = HALO * (k ^ 1)
            back.append(pltpu.roll(four[k], turn, 1) if turn else four[k])
        forward = jnp.where(slot == 0, ahead[0], jnp.where(slot == 1, ahead[1], jnp.where(slot == 2, ahead[2], ahead[3])))
        backward = jnp.where(slot == 0, back[1], jnp.where(slot == 1, back[0], jnp.where(slot == 2, back[3], back[2])))
        forward_ref[lead + (part,)] = forward
        backward_ref[lead + (part,)] = backward


def local_places(neighbours_ref):
    offset = lax.axis_index("surf") * LANES
    found = neighbours_ref[...]
    return found >= 0, found - offset


def own_tables(neighbours_ref, rows):
    valid, local = local_places(neighbours_ref)
    inside = valid & (local >= 0) & (local < LANES)
    lanes = jnp.where(inside, local, 0)
    weight = jnp.where(inside, SURF_WEIGHT * FACE, 0.0)
    return [
        (
            jnp.broadcast_to(lanes[s : s + 1], (rows, LANES)),
            jnp.broadcast_to(weight[s : s + 1], (rows, LANES)),
        )
        for s in range(4)
    ]


def halo_tables(neighbours_ref, rows):
    valid, local = local_places(neighbours_ref)
    low = valid & (local < 0)
    high = valid & (local >= LANES)
    weight = jnp.where(low | high, SURF_WEIGHT * FACE, 0.0)
    tables = []
    for s in range(4):
        lanes = []
        for k in range(4):
            place = jnp.where(low, local + HALO * (k + 1), jnp.where(high, local - LANES + HALO * (k ^ 1), 0))
            lanes.append(jnp.broadcast_to(place[s : s + 1], (rows, LANES)))
        tables.append((lanes, jnp.broadcast_to(weight[s : s + 1], (rows, LANES))))
    return tables


def halo_pair(low, high):
    even = (lane_ids(low.shape[0]) // HALO) % 2 == 0
    return jnp.where(even, low, high), jnp.where(even, high, low)


def absorb_kernel(pops_ref, absorb_ref, emit_ref, energy_ref, source_ref, wall_ref, kappa_ref, emission_ref, forward_ref, backward_ref, edge_ref):
    rows, groups, cells = kappa_ref.shape
    tables = jnp.concatenate([absorb_ref[...], emit_ref[...]], axis=0)
    levels = jnp.swapaxes(pops_ref[...], 0, 1)
    for pair in range(rows // 2):
        both = jnp.concatenate([levels[2 * pair], levels[2 * pair + 1]], axis=1)
        product = jnp.dot(tables, both, preferred_element_type=jnp.float32)
        for k in range(2):
            row = row_of(2 * pair + k, rows)
            kappa_ref[row] = product[:groups, k * cells : (k + 1) * cells]
            emission_ref[row] = product[groups:, k * cells : (k + 1) * cells]

    @pl.when(lax.axis_index("normal") == 0)
    def _():
        kind = wall_ref[...]
        weight = jnp.where(kind == 0, 0.5, jnp.where(kind == 1, 0.25, 0.0))
        source = jnp.broadcast_to(source_ref[...], (groups, groups)).T
        emission_ref[0] = emission_ref[0] + source * weight

    pack_sides([kappa_ref[r] for r in range(rows)], forward_ref, backward_ref, (0,))
    pack_sides(
        [energy_ref[pl.ds(row_of(r, rows), groups, stride=rows), :] for r in range(rows)], forward_ref, backward_ref, (1,)
    )
    edge_ref[...] = kappa_ref[rows - 1]


def own_kernel(kappa_ref, emission_ref, energy_ref, neighbours_ref, wall_ref, base_ref, rhs_ref, face_ref, couple_ref):
    rows, groups, cells = kappa_ref.shape
    chunk = 32
    tables = own_tables(neighbours_ref, chunk)
    kind = wall_ref[...]
    weight = jnp.where(kind == 0, 0.5, jnp.where(kind == 1, 0.25, 0.0))
    boundary = jnp.where(lax.axis_index("normal") == 0, weight, 0.5)

    @pl.loop(0, rows)
    def _(r):
        end = jnp.where(r == 0, boundary, 0.0)
        before = jnp.maximum(r - 1, 0)
        source = row_of(r, rows)
        for part in range(groups // chunk):
            here = pl.ds(part * chunk, chunk)
            kappa = kappa_ref[r, here, :]
            energy = energy_ref[pl.ds(part * chunk * rows + source, chunk, stride=rows), :]
            total = kappa + end
            rhs = emission_ref[r, here, :]
            for s in range(4):
                lanes, factor = tables[s]
                couple = factor * inverse(kappa + gather(kappa, lanes))
                couple_ref[s, r, here, :] = couple
                total = total + couple
                rhs = rhs + couple * gather(energy, lanes)
            base_ref[r, here, :] = total
            rhs_ref[r, here, :] = rhs
            face_ref[r, here, :] = FACE * inverse(kappa_ref[before, here, :] + kappa)


def first_kernel(kappa_ref, base_ref, rhs_ref, face_ref, low_ref, high_ref, neighbours_ref, other_edge_ref, couple_ref, pivot_ref, carried_ref, solved_ref, ends_ref):
    rows, groups, cells = kappa_ref.shape
    chunk = 32
    tables = halo_tables(neighbours_ref, chunk)

    @pl.loop(0, groups // chunk)
    def _(part):
        here = pl.ds(pl.multiple_of(part * chunk, chunk), chunk)
        schur = None
        carried = None
        solved = None
        for r in range(rows):
            quad, k = divmod(r, 4)
            if k == 0:
                halo_kappa = halo_pair(low_ref[0, quad, here, :], high_ref[0, quad, here, :])
                halo_energy = halo_pair(low_ref[1, quad, here, :], high_ref[1, quad, here, :])
            kappa = kappa_ref[r, here, :]
            base = base_ref[r, here, :]
            rhs = rhs_ref[r, here, :]
            for s in range(4):
                lanes, factor = tables[s]
                couple = factor * inverse(kappa + gather(halo_kappa[k % 2], lanes[k]))
                couple_ref[s, r, here, :] = couple
                base = base + couple
                rhs = rhs + couple * gather(halo_energy[k % 2], lanes[k])
            if r > 0:
                face = face_ref[r, here, :]
                base = base + schur * carried
                rhs = rhs + face * solved
            schur = base
            if r == rows - 1:
                ends_ref[0, here, :] = schur
                ends_ref[1, here, :] = rhs
            else:
                after = face_ref[r + 1, here, :]
                pivot = inverse(schur + after)
                carried = after * pivot
                solved = rhs * pivot
                pivot_ref[r, here, :] = pivot
                carried_ref[r, here, :] = carried
                solved_ref[r, here, :] = solved


def meet_kernel(ends_ref, other_ref, edge_ref, other_edge_ref, carried_ref, solved_ref, current_ref, forward_ref, backward_ref, mix_ref):
    rows, groups, cells = current_ref.shape
    face = FACE * inverse(edge_ref[...] + other_edge_ref[...])
    own, other = ends_ref[0], other_ref[0]
    scale = inverse(own * other + face * (own + other))
    near = (other + face) * scale
    far = face * scale
    mix_ref[0] = near
    mix_ref[1] = far
    value = near * ends_ref[1] + far * other_ref[1]
    current_ref[rows - 1] = value
    planes = [value]
    for r in range(rows - 2, -1, -1):
        value = solved_ref[r] + carried_ref[r] * value
        current_ref[r] = value
    pack_sides([current_ref[r] for r in range(rows)], forward_ref, backward_ref, ())


def own_again_kernel(current_ref, emission_ref, couple_ref, neighbours_ref, rhs_ref):
    rows, groups, cells = current_ref.shape
    chunk = 32
    tables = own_tables(neighbours_ref, chunk)

    @pl.loop(0, rows)
    def _(r):
        for part in range(groups // chunk):
            here = pl.ds(part * chunk, chunk)
            current = current_ref[r, here, :]
            rhs = emission_ref[r, here, :]
            for s in range(4):
                rhs = rhs + couple_ref[s, r, here, :] * gather(current, tables[s][0])
            rhs_ref[r, here, :] = rhs


def again_kernel(rhs_ref, low_ref, high_ref, couple_ref, neighbours_ref, pivot_ref, face_ref, solved_ref, end_ref):
    rows, groups, cells = rhs_ref.shape
    chunk = 32
    tables = halo_tables(neighbours_ref, chunk)

    @pl.loop(0, groups // chunk)
    def _(part):
        here = pl.ds(pl.multiple_of(part * chunk, chunk), chunk)
        solved = None
        for r in range(rows):
            quad, k = divmod(r, 4)
            if k == 0:
                halo = halo_pair(low_ref[quad, here, :], high_ref[quad, here, :])
            rhs = rhs_ref[r, here, :]
            for s in range(4):
                rhs = rhs + couple_ref[s, r, here, :] * gather(halo[k % 2], tables[s][0][k])
            if r > 0:
                rhs = rhs + face_ref[r, here, :] * solved
            if r == rows - 1:
                end_ref[here, :] = rhs
            else:
                solved = rhs * pivot_ref[r, here, :]
                solved_ref[r, here, :] = solved


def last_kernel(end_ref, other_ref, mix_ref, carried_ref, solved_ref, out_ref):
    rows = carried_ref.shape[0]
    groups = end_ref.shape[0]
    value = mix_ref[0] * end_ref[...] + mix_ref[1] * other_ref[...]
    out_ref[pl.ds(row_of(rows - 1, rows), groups, stride=rows), :] = value
    for r in range(rows - 2, -1, -1):
        value = solved_ref[r] + carried_ref[r] * value
        out_ref[pl.ds(row_of(r, rows), groups, stride=rows), :] = value


def call(kernel, outs, *args):
    space = pl.BlockSpec(memory_space=pltpu.VMEM)
    return pl.pallas_call(
        kernel,
        out_shape=[jax.ShapeDtypeStruct(shape, jnp.float32) for shape in outs],
        in_specs=[space] * len(args),
        out_specs=[space] * len(outs),
        compiler_params=pltpu.CompilerParams(vmem_limit_bytes=LIMIT),
    )(*args)


def body(populations, absorb_table, emit_table, energy, wall_source, neighbours, wall_type):
    levels, rows, cells = populations.shape
    groups = absorb_table.shape[0]
    whole = (rows, groups, cells)
    plane = (groups, cells)
    packed = (rows // 4, groups, cells)
    count = lax.axis_size("surf")
    ahead = [(i, (i + 1) % count) for i in range(count)]
    back = [(target, source) for source, target in ahead]
    swap = [(0, 1), (1, 0)]
    lines = energy.reshape(groups * rows, cells)
    places = neighbours.T
    walls = wall_type.reshape(1, cells)
    sources = wall_source.reshape(1, groups)

    kappa, emission, forward, backward, edge = call(
        absorb_kernel,
        [whole, whole, (2,) + packed, (2,) + packed, plane],
        populations, absorb_table, emit_table, lines, sources, walls,
    )
    low = lax.ppermute(forward, "surf", ahead)
    high = lax.ppermute(backward, "surf", back)
    other_edge = lax.ppermute(edge, "normal", swap)
    base, rhs, face, own_couple = call(
        own_kernel, [whole, whole, whole, (4,) + whole], kappa, emission, lines, places, walls
    )
    halo_couple, pivot, carried, solved, ends = call(
        first_kernel,
        [(4,) + whole, whole, whole, whole, (2,) + plane],
        kappa, base, rhs, face, low, high, places, other_edge,
    )
    other_ends = lax.ppermute(ends, "normal", swap)
    current, forward, backward, mix = call(
        meet_kernel, [whole, packed, packed, (2,) + plane], ends, other_ends, edge, other_edge, carried, solved
    )
    low = lax.ppermute(forward, "surf", ahead)
    high = lax.ppermute(backward, "surf", back)
    (rhs,) = call(own_again_kernel, [whole], current, emission, own_couple, places)
    solved, end = call(again_kernel, [whole, plane], rhs, low, high, halo_couple, places, pivot, face)
    other_end = lax.ppermute(end, "normal", swap)
    (out,) = call(last_kernel, [(groups * rows, cells)], end, other_end, mix, carried, solved)
    return out.reshape(groups, rows, cells)


def solution(mesh):
    return jax.shard_map(
        body,
        mesh=mesh,
        in_specs=(
            P(None, "normal", "surf"),
            P(),
            P(),
            P(None, "normal", "surf"),
            P(),
            P("surf", None),
            P("surf"),
        ),
        out_specs=P(None, "normal", "surf"),
        check_vma=False,
    )
```

```python
import jax
import jax.numpy as jnp
from jax import lax
from jax.experimental import pallas as pl
from jax.experimental.pallas import tpu as pltpu
from jax.sharding import PartitionSpec as P

HALO = 32
LANES = 128
HALF = 64
SURF_WEIGHT = 0.02
FACE = 2.0 / 3.0
LIMIT = 32 * 1024 * 1024
CHUNK = 32


def inverse(value):
    guess = pl.reciprocal(value, approx=True)
    return guess * (2.0 - value * guess)


def lane_ids(rows):
    return lax.broadcasted_iota(jnp.int32, (rows, LANES), 1)


def gather(value, select):
    high = value.astype(jnp.bfloat16)
    low = (value - high.astype(jnp.float32)).astype(jnp.bfloat16)
    return jnp.dot(jnp.concatenate([high, low], axis=1), select, preferred_element_type=jnp.float32)


def selection(lanes):
    source = lax.broadcasted_iota(jnp.int32, (LANES, LANES), 0)
    parts = [jnp.where(source == lanes[s : s + 1], 1.0, 0.0).astype(jnp.bfloat16) for s in range(4)]
    one = jnp.concatenate(parts, axis=1)
    return jnp.concatenate([one, one], axis=0)


def cut(value, s):
    return value[:, s * LANES : (s + 1) * LANES]


def row_of(position, count):
    block = lax.axis_index("normal")
    return position + block * (count - 1 - 2 * position)


def odd_surf():
    return lax.rem(lax.axis_index("surf"), 2) == 1


def pack_sides(plane_at, rows, far_ref, near_ref):
    groups = far_ref.shape[1]
    slot = lane_ids(groups) // HALO
    odd = odd_surf()
    for part in range(rows // 4):
        four = [plane_at(4 * part + k) for k in range(4)]
        ahead, back = [], []
        for k in range(4):
            turn = (HALO * (k + 1)) % LANES
            ahead.append(pltpu.roll(four[k], turn, 1) if turn else four[k])
            turn = HALO * (k ^ 1)
            back.append(pltpu.roll(four[k], turn, 1) if turn else four[k])
        forward = jnp.where(slot == 0, ahead[0], jnp.where(slot == 1, ahead[1], jnp.where(slot == 2, ahead[2], ahead[3])))
        backward = jnp.where(slot == 0, back[1], jnp.where(slot == 1, back[0], jnp.where(slot == 2, back[3], back[2])))
        far_ref[part] = jnp.where(odd, forward, backward)
        near_ref[part] = jnp.where(odd, backward, forward)


def local_places(neighbours_ref):
    offset = lax.axis_index("surf") * LANES
    found = neighbours_ref[...]
    return found >= 0, found - offset


def spread(table, rows):
    return [jnp.broadcast_to(table[s : s + 1], (rows, LANES)) for s in range(4)]


def edge_lanes(rows):
    lane = lane_ids(rows)
    return (lane < HALO) | (lane >= LANES - HALO)


def own_tables(neighbours_ref):
    valid, local = local_places(neighbours_ref)
    inside = valid & (local >= 0) & (local < LANES)
    return jnp.where(inside, local, -1), jnp.where(inside, SURF_WEIGHT * FACE, 0.0)


def halo_tables(neighbours_ref):
    valid, local = local_places(neighbours_ref)
    low = valid & (local < 0)
    high = valid & (local >= LANES)
    edge = edge_lanes(4)
    weight = jnp.where(low | high, SURF_WEIGHT * FACE, 0.0)
    weight = jnp.where(edge, weight, pltpu.roll(weight, HALF, 1))
    lanes = []
    for k in range(2):
        place = jnp.where(low, local + HALO * (k + 1), jnp.where(high, local - LANES + HALO * (k ^ 1), -LANES))
        lanes.append(jnp.where(edge, place, pltpu.roll(place, HALF, 1) + HALF))
    return lanes, weight


def halo_pair(far, near):
    even = (lane_ids(far.shape[0]) // HALO) % 2 == 0
    first = even != odd_surf()
    return jnp.where(first, far, near), jnp.where(first, near, far)


def start_kernel(pops_hbm, absorb_hbm, emit_hbm, energy_hbm, source_hbm, wall_hbm, kappa_ref, emission_ref, current_ref, far_ref, near_ref, edge_ref, pops_ref, table_ref, lines_ref, source_ref, wall_ref, sems):
    rows, groups, cells = kappa_ref.shape
    levels = pops_ref.shape[0]
    pieces = 4
    first, later = [], []
    step = levels // pieces
    for piece in range(pieces):
        here = pl.ds(piece * step, step)
        first.append(pltpu.make_async_copy(pops_hbm.at[here], pops_ref.at[here], sems.at[piece]))
    first.append(pltpu.make_async_copy(absorb_hbm, table_ref.at[pl.ds(0, groups)], sems.at[pieces]))
    first.append(pltpu.make_async_copy(emit_hbm, table_ref.at[pl.ds(groups, groups)], sems.at[pieces + 1]))
    later.append(pltpu.make_async_copy(source_hbm, source_ref, sems.at[pieces + 2]))
    later.append(pltpu.make_async_copy(wall_hbm, wall_ref, sems.at[pieces + 3]))
    step = groups * rows // pieces
    for piece in range(pieces):
        here = pl.ds(piece * step, step)
        later.append(pltpu.make_async_copy(energy_hbm.at[here], lines_ref.at[here], sems.at[pieces + 4 + piece]))
    for copy in first + later:
        copy.start()
    for copy in first:
        copy.wait()
    table = table_ref[...]
    turned = jnp.swapaxes(pops_ref[...], 0, 1)
    for pair in range(rows // 2):
        both = jnp.concatenate([turned[2 * pair], turned[2 * pair + 1]], axis=1)
        product = jnp.dot(table, both, preferred_element_type=jnp.float32)
        for k in range(2):
            row = row_of(2 * pair + k, rows)
            kappa_ref[row] = product[:groups, k * cells : (k + 1) * cells]
            emission_ref[row] = product[groups:, k * cells : (k + 1) * cells]
    for copy in later:
        copy.wait()

    @pl.when(lax.axis_index("normal") == 0)
    def _():
        kind = wall_ref[...]
        weight = jnp.where(kind == 0, 0.5, jnp.where(kind == 1, 0.25, 0.0))
        source = jnp.broadcast_to(source_ref[...], (groups, groups)).T
        emission_ref[0] = emission_ref[0] + source * weight

    pack_sides(lambda r: kappa_ref[r], rows, far_ref.at[0], near_ref.at[0])
    edge_ref[...] = kappa_ref[rows - 1]
    for r in range(rows):
        current_ref[r] = lines_ref[pl.ds(row_of(r, rows), groups, stride=rows), :]
    pack_sides(lambda r: current_ref[r], rows, far_ref.at[1], near_ref.at[1])


def own_kernel(kappa_ref, emission_ref, current_ref, neighbours_ref, wall_ref, base_ref, face_ref, couple_ref, paired_ref, rhs_ref, select_ref):
    rows, groups, cells = kappa_ref.shape
    lanes, weight = own_tables(neighbours_ref)
    select = selection(lanes)
    weight = spread(weight, groups)
    kind = wall_ref[...]
    share = jnp.where(kind == 0, 0.5, jnp.where(kind == 1, 0.25, 0.0))
    boundary = jnp.where(lax.axis_index("normal") == 0, share, 0.5)

    @pl.loop(0, rows // 4)
    def _(quad):
        here = pl.ds(quad * 4, 4)
        planes = jnp.concatenate([kappa_ref[here], current_ref[here]], axis=0).reshape(8 * groups, cells)
        found = gather(planes, select)
        for k in range(4):
            r = quad * 4 + k
            kappa = kappa_ref[r]
            total = kappa + jnp.where(r == 0, boundary, 0.0) if k == 0 else kappa
            rhs = emission_ref[r]
            near_kappa = found[k * groups : (k + 1) * groups]
            near_current = found[(4 + k) * groups : (5 + k) * groups]
            for s in range(4):
                couple = weight[s] * inverse(kappa + cut(near_kappa, s))
                couple_ref[s, r] = couple
                total = total + couple
                rhs = rhs + couple * cut(near_current, s)
            base_ref[r] = total
            rhs_ref[r] = rhs
            face_ref[r] = FACE * inverse(kappa_ref[jnp.maximum(r - 1, 0)] + kappa)

    edge = edge_lanes(groups)
    for pair in range(rows // 2):
        quad, k = divmod(pair, 2)
        paired_ref[pair] = jnp.where(edge, kappa_ref[4 * quad + k], pltpu.roll(kappa_ref[4 * quad + k + 2], HALF, 1))
    lanes, weight = halo_tables(neighbours_ref)
    for k in range(2):
        select_ref[k] = selection(lanes[k])


def first_kernel(base_ref, face_ref, rhs_ref, paired_ref, edge_ref, other_edge_ref, far_ref, near_ref, neighbours_ref, select_ref, couple_ref, pivot_ref, carried_ref, solved_ref, ends_ref, meeting_ref, found_ref):
    rows, groups, cells = base_ref.shape
    meeting_ref[...] = FACE * inverse(edge_ref[...] + other_edge_ref[...])
    lanes, weight = halo_tables(neighbours_ref)
    weight = spread(weight, CHUNK)
    quads = rows // 4
    far = far_ref[...].reshape(2 * quads * groups, cells)
    near = near_ref[...].reshape(2 * quads * groups, cells)
    halo = halo_pair(far, near)
    for k in range(2):
        found_ref[k] = gather(halo[k], select_ref[k])
    edge = edge_lanes(CHUNK)

    @pl.loop(0, groups // CHUNK)
    def _(part):
        start = pl.multiple_of(part * CHUNK, CHUNK)
        here = pl.ds(start, CHUNK)
        schur = None
        carried = None
        solved = None
        for quad in range(quads):
            sums, terms = [], []
            for k in range(2):
                pair = 2 * quad + k
                kappa = paired_ref[pair, here, :]
                near_kappa = found_ref[k, pl.ds(quad * groups + start, CHUNK), :]
                near_current = found_ref[k, pl.ds((quads + quad) * groups + start, CHUNK), :]
                total = None
                for s in range(4):
                    couple = weight[s] * inverse(kappa + cut(near_kappa, s))
                    couple_ref[s, pair, here, :] = couple
                    term = couple * cut(near_current, s)
                    total = couple if s == 0 else total + couple
                    extra = term if s == 0 else extra + term
                sums.append(total)
                terms.append(extra)
            for k in range(4):
                r = 4 * quad + k
                extra = sums[k] if k < 2 else pltpu.roll(sums[k - 2], HALF, 1)
                base = base_ref[r, here, :] + jnp.where(edge, extra, 0.0)
                extra = terms[k] if k < 2 else pltpu.roll(terms[k - 2], HALF, 1)
                rhs = rhs_ref[r, here, :] + jnp.where(edge, extra, 0.0)
                if r == 0:
                    schur = base
                else:
                    schur = base + schur * carried
                    rhs = rhs + face_ref[r, here, :] * solved
                if r == rows - 1:
                    ends_ref[0, here, :] = schur
                    ends_ref[1, here, :] = rhs
                else:
                    after = face_ref[r + 1, here, :]
                    pivot = inverse(schur + after)
                    carried = after * pivot
                    solved = rhs * pivot
                    pivot_ref[r, here, :] = pivot
                    carried_ref[r, here, :] = carried
                    solved_ref[r, here, :] = solved


def again_kernel(rhs_ref, far_ref, near_ref, couple_ref, select_ref, pivot_ref, face_ref, solved_ref, end_ref, found_ref):
    rows, groups, cells = rhs_ref.shape
    quads = rows // 4
    halo = halo_pair(far_ref[...].reshape(quads * groups, cells), near_ref[...].reshape(quads * groups, cells))
    for k in range(2):
        found_ref[k] = gather(halo[k], select_ref[k])
    edge = edge_lanes(CHUNK)

    @pl.loop(0, groups // CHUNK)
    def _(part):
        start = pl.multiple_of(part * CHUNK, CHUNK)
        here = pl.ds(start, CHUNK)
        solved = None
        for quad in range(quads):
            terms = []
            for k in range(2):
                near_current = found_ref[k, pl.ds(quad * groups + start, CHUNK), :]
                total = None
                for s in range(4):
                    term = couple_ref[s, 2 * quad + k, here, :] * cut(near_current, s)
                    total = term if s == 0 else total + term
                terms.append(total)
            for k in range(4):
                r = 4 * quad + k
                extra = terms[k] if k < 2 else pltpu.roll(terms[k - 2], HALF, 1)
                rhs = rhs_ref[r, here, :] + jnp.where(edge, extra, 0.0)
                if r > 0:
                    rhs = rhs + face_ref[r, here, :] * solved
                if r == rows - 1:
                    end_ref[here, :] = rhs
                else:
                    solved = rhs * pivot_ref[r, here, :]
                    solved_ref[r, here, :] = solved


def meet_kernel(ends_ref, other_ref, meeting_ref, carried_ref, solved_ref, current_ref, far_ref, near_ref, mix_ref):
    rows, groups, cells = current_ref.shape
    face = meeting_ref[...]
    own, other = ends_ref[0], other_ref[0]
    scale = inverse(own * other + face * (own + other))
    mine = (other + face) * scale
    theirs = face * scale
    mix_ref[0] = mine
    mix_ref[1] = theirs
    value = mine * ends_ref[1] + theirs * other_ref[1]
    current_ref[rows - 1] = value
    for r in range(rows - 2, -1, -1):
        value = solved_ref[r] + carried_ref[r] * value
        current_ref[r] = value
    pack_sides(lambda r: current_ref[r], rows, far_ref, near_ref)


def own_again_kernel(current_ref, emission_ref, couple_ref, neighbours_ref, rhs_ref):
    rows, groups, cells = current_ref.shape
    lanes, weight = own_tables(neighbours_ref)
    select = selection(lanes)

    @pl.loop(0, rows // 4)
    def _(quad):
        found = gather(current_ref[pl.ds(quad * 4, 4)].reshape(4 * groups, cells), select)
        for k in range(4):
            r = quad * 4 + k
            rhs = emission_ref[r]
            for s in range(4):
                rhs = rhs + couple_ref[s, r] * cut(found[k * groups : (k + 1) * groups], s)
            rhs_ref[r] = rhs


def last_kernel(end_ref, other_ref, mix_ref, carried_ref, solved_ref, out_hbm, lines_ref, sems):
    rows, groups, cells = carried_ref.shape
    copies = []
    for part in range(groups // CHUNK):
        start = part * CHUNK
        here = pl.ds(start, CHUNK)
        value = mix_ref[0, here, :] * end_ref[here, :] + mix_ref[1, here, :] * other_ref[here, :]
        lines_ref[pl.ds(start * rows + row_of(rows - 1, rows), CHUNK, stride=rows), :] = value
        for r in range(rows - 2, -1, -1):
            value = solved_ref[r, here, :] + carried_ref[r, here, :] * value
            lines_ref[pl.ds(start * rows + row_of(r, rows), CHUNK, stride=rows), :] = value
        there = pl.ds(start * rows, CHUNK * rows)
        copies.append(pltpu.make_async_copy(lines_ref.at[there], out_hbm.at[there], sems.at[part]))
        copies[-1].start()
    for copy in copies:
        copy.wait()


VMEM = pl.BlockSpec(memory_space=pltpu.VMEM)
HBM = pl.BlockSpec(memory_space=pltpu.HBM)


def call(kernel, outs, *args, space=VMEM, out_space=VMEM, scratch=()):
    return pl.pallas_call(
        kernel,
        out_shape=[jax.ShapeDtypeStruct(out, jnp.float32) if isinstance(out, tuple) else out for out in outs],
        in_specs=[space] * len(args),
        out_specs=[out_space] * len(outs),
        scratch_shapes=list(scratch),
        compiler_params=pltpu.CompilerParams(vmem_limit_bytes=LIMIT),
    )(*args)


def body(populations, absorb_table, emit_table, energy, wall_source, neighbours, wall_type):
    levels, rows, cells = populations.shape
    groups = absorb_table.shape[0]
    whole = (rows, groups, cells)
    plane = (groups, cells)
    packed = (rows // 4, groups, cells)
    pairs = (rows // 2, groups, cells)
    count = lax.axis_size("surf")
    far = [(i, (i + 1) % count if i % 2 else (i - 1) % count) for i in range(count)]
    near = [(i, i ^ 1) for i in range(count)]
    swap = [(0, 1), (1, 0)]
    lines = energy.reshape(groups * rows, cells)
    places = neighbours.T
    walls = wall_type.reshape(1, cells)
    sources = wall_source.reshape(1, groups)

    def halo(far_side, near_side):
        near_side = lax.ppermute(near_side, "surf", near)
        return lax.ppermute(far_side, "surf", far), near_side

    inputs = (populations, absorb_table, emit_table, lines, sources, walls)
    kappa, emission, current, far_side, near_side, edge = call(
        start_kernel,
        [whole, whole, whole, (2,) + packed, (2,) + packed, plane],
        *[pltpu.with_memory_space_constraint(value, pltpu.HBM) for value in inputs],
        space=HBM,
        scratch=[
            pltpu.VMEM(populations.shape, populations.dtype),
            pltpu.VMEM((2 * groups, levels), absorb_table.dtype),
            pltpu.VMEM(lines.shape, jnp.float32),
            pltpu.VMEM((1, groups), jnp.float32),
            pltpu.VMEM((1, cells), jnp.int32),
            pltpu.SemaphoreType.DMA((12,)),
        ],
    )
    far_side, near_side = halo(far_side, near_side)
    other_edge = lax.ppermute(edge, "normal", swap)
    base, face, own_couple, paired, rhs, select = call(
        own_kernel,
        [whole, whole, (4,) + whole, pairs, whole, jax.ShapeDtypeStruct((2, 2 * LANES, 4 * LANES), jnp.bfloat16)],
        kappa, emission, current, places, walls,
    )
    halo_couple, pivot, carried, solved, ends, meeting = call(
        first_kernel,
        [(4,) + pairs, whole, whole, whole, (2,) + plane, plane],
        base, face, rhs, paired, edge, other_edge, far_side, near_side, places, select,
        scratch=[pltpu.VMEM((2, 2 * packed[0] * groups, 4 * LANES), jnp.float32)],
    )
    other_ends = lax.ppermute(ends, "normal", swap)
    current, far_side, near_side, mix = call(
        meet_kernel, [whole, packed, packed, (2,) + plane], ends, other_ends, meeting, carried, solved
    )
    far_side, near_side = halo(far_side, near_side)
    (rhs,) = call(own_again_kernel, [whole], current, emission, own_couple, places)
    solved, end = call(
        again_kernel, [whole, plane], rhs, far_side, near_side, halo_couple, select, pivot, face,
        scratch=[pltpu.VMEM((2, packed[0] * groups, 4 * LANES), jnp.float32)],
    )
    other_end = lax.ppermute(end, "normal", swap)
    (out,) = call(
        last_kernel, [lines.shape], end, other_end, mix, carried, solved,
        out_space=HBM,
        scratch=[pltpu.VMEM(lines.shape, jnp.float32), pltpu.SemaphoreType.DMA((groups // CHUNK,))],
    )
    return out.reshape(groups, rows, cells)


def solution(mesh):
    return jax.shard_map(
        body,
        mesh=mesh,
        in_specs=(
            P(None, "normal", "surf"),
            P(),
            P(),
            P(None, "normal", "surf"),
            P(),
            P("surf", None),
            P("surf"),
        ),
        out_specs=P(None, "normal", "surf"),
        check_vma=False,
    )
```

```python
import jax
import jax.numpy as jnp
from jax import lax
from jax.experimental import pallas as pl
from jax.experimental.pallas import tpu as pltpu
from jax.sharding import PartitionSpec as P

HALO = 32
LANES = 128
HALF = 64
SURF_WEIGHT = 0.02
FACE = 2.0 / 3.0
LIMIT = 32 * 1024 * 1024
CHUNK = 64


def inverse(value):
    guess = pl.reciprocal(value, approx=True)
    return guess * (2.0 - value * guess)


def lane_ids(rows):
    return lax.broadcasted_iota(jnp.int32, (rows, LANES), 1)


def gather(value, select):
    high = value.astype(jnp.bfloat16)
    low = (value - high.astype(jnp.float32)).astype(jnp.bfloat16)
    return jnp.dot(jnp.concatenate([high, low], axis=1), select, preferred_element_type=jnp.float32)


def selection(lanes):
    source = lax.broadcasted_iota(jnp.int32, (LANES, LANES), 0)
    parts = [jnp.where(source == lanes[s : s + 1], 1.0, 0.0).astype(jnp.bfloat16) for s in range(4)]
    one = jnp.concatenate(parts, axis=1)
    return jnp.concatenate([one, one], axis=0)


def cut(value, s):
    return value[:, s * LANES : (s + 1) * LANES]


def row_of(position, count):
    block = lax.axis_index("normal")
    return position + block * (count - 1 - 2 * position)


def odd_surf():
    return lax.rem(lax.axis_index("surf"), 2)


def pack(plane, high):
    slot = lane_ids(HALO) // HALO
    packed = None
    for k in range(4):
        turned = pltpu.roll(plane[k * HALO : (k + 1) * HALO], HALO * lax.rem(k + high, 4), 1)
        packed = turned if k == 0 else jnp.where(slot == k, turned, packed)
    return packed


def local_places(neighbours_ref):
    offset = lax.axis_index("surf") * LANES
    found = neighbours_ref[...]
    return found >= 0, found - offset


def spread(table, rows):
    return [jnp.broadcast_to(table[s : s + 1], (rows, LANES)) for s in range(4)]


def own_tables(neighbours_ref):
    valid, local = local_places(neighbours_ref)
    inside = valid & (local >= 0) & (local < LANES)
    return jnp.where(inside, local, -1), jnp.where(inside, SURF_WEIGHT * FACE, 0.0)


def side_tables(neighbours_ref, high):
    valid, local = local_places(neighbours_ref)
    slot = lane_ids(4) // HALO
    place = local + (HALO - high * (LANES + HALO))
    here = slot == 3 * high
    beyond = valid & here & (place >= 0) & (place < HALO)
    place = jnp.where(beyond, place, -LANES)
    weight = jnp.where(beyond, SURF_WEIGHT * FACE, 0.0)

    def repeat(value):
        value = jnp.where(here, value, 0)
        return value + pltpu.roll(value, HALO, 1) + pltpu.roll(value, 2 * HALO, 1) + pltpu.roll(value, 3 * HALO, 1)

    return repeat(place) + HALO * slot, repeat(weight)


def unpack(value, high, quarters=range(4)):
    here = lane_ids(HALO) // HALO == 3 * high
    return jnp.concatenate(
        [jnp.where(here, pltpu.roll(value, HALO * lax.rem(4 - k - high, 4), 1), 0.0) for k in quarters], axis=0
    )


def kappa_kernel(pops_hbm, absorb_hbm, emit_hbm, lines_hbm, places_hbm, walls_hbm, sources_hbm, kappa_ref, turned_ref, far_ref, edge_ref, emit_ref, lines_ref, places_ref, walls_ref, sources_ref, pops_ref, table_ref, sems):
    rows, groups, cells = kappa_ref.shape
    levels = pops_ref.shape[0]
    pieces = 4
    step = levels // pieces
    pairs = []
    for piece in range(pieces):
        here = pl.ds(piece * step, step)
        pairs.append((pops_hbm.at[here], pops_ref.at[here]))
    pairs.append((absorb_hbm, table_ref))
    step = groups * rows // pieces
    for piece in range(pieces):
        there = pl.ds(piece * step, step)
        pairs.append((lines_hbm.at[there], lines_ref.at[there]))
    pairs += [(emit_hbm, emit_ref), (places_hbm, places_ref), (walls_hbm, walls_ref), (sources_hbm, sources_ref)]
    copies = [pltpu.make_async_copy(pair[0], pair[1], sems.at[i]) for i, pair in enumerate(pairs)]
    for copy in copies:
        copy.start()
    step = levels // pieces
    for piece in range(pieces):
        copies[piece].wait()
        here = pl.ds(piece * step, step)
        turned_ref[:, here, :] = jnp.swapaxes(pops_ref[here], 0, 1)
    copies[pieces].wait()
    table = table_ref[...]
    for pair in range(rows // 2):
        both = jnp.concatenate([turned_ref[2 * pair], turned_ref[2 * pair + 1]], axis=1)
        product = jnp.dot(table, both, preferred_element_type=jnp.float32)
        for k in range(2):
            kappa_ref[row_of(2 * pair + k, rows)] = product[:, k * cells : (k + 1) * cells]
    odd = odd_surf()
    for r in range(rows):
        far_ref[0, r] = pack(kappa_ref[r], odd)
    edge_ref[...] = kappa_ref[rows - 1]
    for copy in copies[pieces + 1 :]:
        copy.wait()
    for r in range(rows):
        far_ref[1, r] = pack(lines_ref[pl.ds(row_of(r, rows), groups, stride=rows), :], odd)


def near_kernel(lines_ref, kappa_ref, current_ref, near_kappa_ref, *half_refs):
    rows, groups, cells = current_ref.shape
    low_near = 1 - odd_surf()
    for r in range(rows):
        current = lines_ref[pl.ds(row_of(r, rows), groups, stride=rows), :]
        current_ref[r] = current
        side = pack(kappa_ref[r], low_near)
        near_kappa_ref[r] = side
        half_refs[r // 8][r % 8] = side
        half_refs[2 + r // 8][r % 8] = pack(current, low_near)


def own_kernel(kappa_ref, current_ref, near_kappa_0, near_kappa_1, near_current_0, near_current_1, mine_ref, turned_ref, emit_ref, source_ref, neighbours_ref, wall_ref, base_ref, face_ref, emission_ref, rhs_ref, couple_ref, near_couple_ref, select_ref, weight_ref, beside_ref):
    rows, groups, cells = kappa_ref.shape
    high = odd_surf()
    low_near = 1 - high
    lanes, weight = side_tables(neighbours_ref, high)
    select_ref[2] = selection(lanes)
    weight_ref[...] = weight
    lanes, weight = own_tables(neighbours_ref)
    select_ref[0] = selection(lanes)
    weight = spread(weight, groups)
    lanes, near_weight = side_tables(neighbours_ref, low_near)
    select_ref[1] = selection(lanes)
    near_weight = spread(near_weight, HALO)
    halves = [near_kappa_0[...], near_kappa_1[...], near_current_0[...], near_current_1[...]]
    halves = jnp.concatenate(halves, axis=0).reshape(2 * rows * HALO, cells)
    beside_ref[...] = gather(halves, select_ref[1]).reshape(beside_ref.shape)
    kind = wall_ref[...]
    share = jnp.where(kind == 0, 0.5, jnp.where(kind == 1, 0.25, 0.0))
    at_wall = lax.axis_index("normal") == 0
    boundary = jnp.where(at_wall, share, 0.5)
    source = jnp.broadcast_to(source_ref[...], (groups, groups)).T * jnp.where(at_wall, share, 0.0)
    table = emit_ref[...]
    for pair in range(rows // 2):
        both = jnp.concatenate([turned_ref[2 * pair], turned_ref[2 * pair + 1]], axis=1)
        product = jnp.dot(table, both, preferred_element_type=jnp.float32)
        for k in range(2):
            emission_ref[row_of(2 * pair + k, rows)] = product[:, k * cells : (k + 1) * cells]
    emission_ref[0] = emission_ref[0] + source

    @pl.loop(0, rows // 4)
    def _(quad):
        here = pl.ds(quad * 4, 4)
        planes = jnp.concatenate([kappa_ref[here], current_ref[here]], axis=0).reshape(8 * groups, cells)
        found = gather(planes, select_ref[0])
        for k in range(4):
            r = quad * 4 + k
            kappa = mine_ref[r]
            for s in range(4):
                couple = near_weight[s] * inverse(kappa + cut(beside_ref[0, r], s))
                near_couple_ref[s, r] = couple
                term = couple * cut(beside_ref[1, r], s)
                near_total = couple if s == 0 else near_total + couple
                near_term = term if s == 0 else near_term + term
            kappa = kappa_ref[r]
            total = kappa + unpack(near_total, low_near)
            if k == 0:
                total = total + jnp.where(r == 0, boundary, 0.0)
            rhs = emission_ref[r] + unpack(near_term, low_near)
            for s in range(4):
                couple = weight[s] * inverse(kappa + cut(found[k * groups : (k + 1) * groups], s))
                couple_ref[s, r] = couple
                total = total + couple
                rhs = rhs + couple * cut(found[(4 + k) * groups : (5 + k) * groups], s)
            base_ref[r] = total
            rhs_ref[r] = rhs
            face_ref[r] = FACE * inverse(kappa_ref[jnp.maximum(r - 1, 0)] + kappa)


def own_again_kernel(current_ref, near_ref, emission_ref, couple_ref, near_couple_ref, select_ref, rhs_ref, beside_ref):
    rows, groups, cells = current_ref.shape
    low_near = 1 - odd_surf()
    beside_ref[...] = gather(near_ref[low_near].reshape(rows * HALO, cells), select_ref[1]).reshape(beside_ref.shape)

    @pl.loop(0, rows // 4)
    def _(quad):
        found = gather(current_ref[pl.ds(quad * 4, 4)].reshape(4 * groups, cells), select_ref[0])
        for k in range(4):
            r = quad * 4 + k
            for s in range(4):
                term = near_couple_ref[s, r] * cut(beside_ref[r], s)
                near_term = term if s == 0 else near_term + term
            rhs = emission_ref[r] + unpack(near_term, low_near)
            for s in range(4):
                rhs = rhs + couple_ref[s, r] * cut(found[k * groups : (k + 1) * groups], s)
            rhs_ref[r] = rhs


def halo_terms(halo_ref, couple_ref, select_ref, found_ref, total_ref):
    rows = total_ref.shape[0]
    found_ref[...] = gather(halo_ref[...].reshape(rows * HALO, LANES), select_ref[2]).reshape(found_ref.shape)
    for r in range(rows):
        total = None
        for s in range(4):
            term = couple_ref[s, r] * cut(found_ref[r], s)
            total = term if s == 0 else total + term
        total_ref[r] = total


def first_kernel(base_ref, face_ref, rhs_ref, mine_ref, far_ref, select_ref, weight_ref, edge_ref, other_edge_ref, couple_ref, pivot_ref, carried_ref, solved_ref, ends_ref, meeting_ref, found_ref, total_ref, term_ref):
    rows, groups, cells = base_ref.shape
    meeting_ref[...] = FACE * inverse(edge_ref[...] + other_edge_ref[...])
    high = odd_surf()
    found_ref[...] = gather(far_ref[...].reshape(2 * rows * HALO, cells), select_ref[2]).reshape(found_ref.shape)
    weight = spread(weight_ref[...], HALO)
    for r in range(rows):
        kappa = mine_ref[0, r]
        for s in range(4):
            couple = weight[s] * inverse(kappa + cut(found_ref[r], s))
            couple_ref[s, r] = couple
            term = couple * cut(found_ref[rows + r], s)
            total = couple if s == 0 else total + couple
            terms = term if s == 0 else terms + term
        total_ref[r] = total
        term_ref[r] = terms

    @pl.loop(0, groups // CHUNK)
    def _(part):
        here = pl.ds(pl.multiple_of(part * CHUNK, CHUNK), CHUNK)
        quarters = [part * (CHUNK // HALO) + k for k in range(CHUNK // HALO)]
        schur = None
        carried = None
        solved = None
        for r in range(rows):
            base = base_ref[r, here, :] + unpack(total_ref[r], high, quarters)
            rhs = rhs_ref[r, here, :] + unpack(term_ref[r], high, quarters)
            if r == 0:
                schur = base
            else:
                schur = base + schur * carried
                rhs = rhs + face_ref[r, here, :] * solved
            if r == rows - 1:
                ends_ref[0, here, :] = schur
                ends_ref[1, here, :] = rhs
            else:
                after = face_ref[r + 1, here, :]
                pivot = inverse(schur + after)
                carried = after * pivot
                solved = rhs * pivot
                pivot_ref[r, here, :] = pivot
                carried_ref[r, here, :] = carried
                solved_ref[r, here, :] = solved


def meet_kernel(ends_ref, other_ref, meeting_ref, carried_ref, solved_ref, current_ref, far_ref, mix_ref):
    rows, groups, cells = current_ref.shape
    odd = odd_surf()
    face = meeting_ref[...]
    own, other = ends_ref[0], other_ref[0]
    scale = inverse(own * other + face * (own + other))
    mine = (other + face) * scale
    theirs = face * scale
    mix_ref[0] = mine
    mix_ref[1] = theirs
    value = mine * ends_ref[1] + theirs * other_ref[1]
    current_ref[rows - 1] = value
    far_ref[rows - 1] = pack(value, odd)
    for r in range(rows - 2, -1, -1):
        value = solved_ref[r] + carried_ref[r] * value
        current_ref[r] = value
        far_ref[r] = pack(value, odd)


def near_again_kernel(current_ref, near_ref):
    low_near = 1 - odd_surf()
    for r in range(current_ref.shape[0]):
        near_ref[r] = pack(current_ref[r], low_near)


def again_kernel(rhs_ref, far_ref, couple_ref, select_ref, pivot_ref, face_ref, solved_ref, end_ref, found_ref, total_ref):
    rows, groups, cells = rhs_ref.shape
    high = odd_surf()
    halo_terms(far_ref, couple_ref, select_ref, found_ref, total_ref)

    @pl.loop(0, groups // CHUNK)
    def _(part):
        here = pl.ds(pl.multiple_of(part * CHUNK, CHUNK), CHUNK)
        quarters = [part * (CHUNK // HALO) + k for k in range(CHUNK // HALO)]
        solved = None
        for r in range(rows):
            rhs = rhs_ref[r, here, :] + unpack(total_ref[r], high, quarters)
            if r > 0:
                rhs = rhs + face_ref[r, here, :] * solved
            if r == rows - 1:
                end_ref[here, :] = rhs
            else:
                solved = rhs * pivot_ref[r, here, :]
                solved_ref[r, here, :] = solved


def last_kernel(end_ref, other_ref, mix_ref, carried_ref, solved_ref, out_hbm, lines_ref, sems):
    rows, groups, cells = carried_ref.shape
    copies = []
    step = groups // 4
    for part in range(4):
        start = part * step
        here = pl.ds(start, step)
        value = mix_ref[0, here, :] * end_ref[here, :] + mix_ref[1, here, :] * other_ref[here, :]
        lines_ref[pl.ds(start * rows + row_of(rows - 1, rows), step, stride=rows), :] = value
        for r in range(rows - 2, -1, -1):
            value = solved_ref[r, here, :] + carried_ref[r, here, :] * value
            lines_ref[pl.ds(start * rows + row_of(r, rows), step, stride=rows), :] = value
        there = pl.ds(start * rows, step * rows)
        copies.append(pltpu.make_async_copy(lines_ref.at[there], out_hbm.at[there], sems.at[part]))
        copies[-1].start()
    for copy in copies:
        copy.wait()


VMEM = pl.BlockSpec(memory_space=pltpu.VMEM)
HBM = pl.BlockSpec(memory_space=pltpu.HBM)


def call(kernel, outs, *args, space=VMEM, out_space=VMEM, scratch=()):
    return pl.pallas_call(
        kernel,
        out_shape=[jax.ShapeDtypeStruct(out, jnp.float32) if isinstance(out, tuple) else out for out in outs],
        in_specs=[space] * len(args),
        out_specs=[out_space] * len(outs),
        scratch_shapes=list(scratch),
        compiler_params=pltpu.CompilerParams(vmem_limit_bytes=LIMIT),
    )(*args)


def like(value):
    return jax.ShapeDtypeStruct(value.shape, value.dtype)


def in_hbm(*values):
    return [pltpu.with_memory_space_constraint(value, pltpu.HBM) for value in values]


def far_pairs(count):
    pairs = []
    for block in range(2):
        for i in range(count):
            if i in (0, count - 1):
                pairs.append((block * count + i, (1 - block) * count + count - 1 - i))
            else:
                pairs.append((block * count + i, block * count + (i + 1 if i % 2 else i - 1)))
    return pairs


def body(populations, absorb_table, emit_table, energy, wall_source, neighbours, wall_type):
    levels, rows, cells = populations.shape
    groups = absorb_table.shape[0]
    whole = (rows, groups, cells)
    plane = (groups, cells)
    side = (rows, HALO, cells)
    found = pltpu.VMEM((rows, HALO, 4 * LANES), jnp.float32)
    found_both = pltpu.VMEM((2 * rows, HALO, 4 * LANES), jnp.float32)
    sums = pltpu.VMEM(side, jnp.float32)
    count = lax.axis_size("surf")
    far = far_pairs(count)
    near = [[i, i + 1] for i in range(0, count, 2)]
    swap = [(0, 1), (1, 0)]
    lines = energy.reshape(groups * rows, cells)
    places = neighbours.T
    walls = wall_type.reshape(1, cells)
    sources = wall_source.reshape(1, groups)

    kappa, turned, mine, edge, emit, lines, places, walls, sources = call(
        kappa_kernel,
        [
            whole, jax.ShapeDtypeStruct((rows, levels, cells), populations.dtype), (2,) + side, plane,
            like(emit_table), like(lines), like(places), like(walls), like(sources),
        ],
        *in_hbm(populations, absorb_table, emit_table, lines, places, walls, sources),
        space=HBM,
        scratch=[
            pltpu.VMEM(populations.shape, populations.dtype),
            pltpu.VMEM(absorb_table.shape, absorb_table.dtype),
            pltpu.SemaphoreType.DMA((13,)),
        ],
    )
    far_both = lax.ppermute(mine, ("normal", "surf"), far)
    other_edge = lax.ppermute(edge, "normal", swap)
    current, near_kappa, *halves = call(near_kernel, [whole, side] + [(rows // 2, HALO, cells)] * 4, lines, kappa)
    halves = [lax.ppermute(half, "surf", [(i, i ^ 1) for i in range(count)]) for half in halves]
    base, face, emission, rhs, own_couple, near_couple, select, weight = call(
        own_kernel,
        [
            whole, whole, whole, whole, (4,) + whole, (4,) + side,
            jax.ShapeDtypeStruct((3, 2 * LANES, 4 * LANES), jnp.bfloat16), (4, LANES),
        ],
        kappa, current, *halves, near_kappa, turned, emit, sources, places, walls,
        scratch=[pltpu.VMEM((2, rows, HALO, 4 * LANES), jnp.float32)],
    )
    far_couple, pivot, carried, solved, ends, meeting = call(
        first_kernel, [(4,) + side, whole, whole, whole, (2,) + plane, plane],
        base, face, rhs, mine, far_both, select, weight, edge, other_edge,
        scratch=[found_both, sums, sums],
    )
    other_ends = lax.ppermute(ends, "normal", swap)
    current, far_mine, mix = call(
        meet_kernel, [whole, side, (2,) + plane], ends, other_ends, meeting, carried, solved
    )
    far_current = lax.ppermute(far_mine, ("normal", "surf"), far)
    (near_mine,) = call(near_again_kernel, [side], current)
    beside = lax.all_gather(near_mine, "surf", axis_index_groups=near)
    (rhs,) = call(
        own_again_kernel, [whole], current, beside, emission, own_couple, near_couple, select, scratch=[found]
    )
    solved, end = call(
        again_kernel, [whole, plane], rhs, far_current, far_couple, select, pivot, face, scratch=[found, sums]
    )
    other_end = lax.ppermute(end, "normal", swap)
    (out,) = call(
        last_kernel, [lines.shape], end, other_end, mix, carried, solved,
        out_space=HBM,
        scratch=[pltpu.VMEM(lines.shape, jnp.float32), pltpu.SemaphoreType.DMA((4,))],
    )
    return out.reshape(groups, rows, cells)


def solution(mesh):
    return jax.shard_map(
        body,
        mesh=mesh,
        in_specs=(
            P(None, "normal", "surf"),
            P(),
            P(),
            P(None, "normal", "surf"),
            P(),
            P("surf", None),
            P("surf"),
        ),
        out_specs=P(None, "normal", "surf"),
        check_vma=False,
    )
```

```python
import functools

import jax
import jax.numpy as jnp
from jax import lax
from jax.experimental import pallas as pl
from jax.experimental.pallas import tpu as pltpu
from jax.sharding import PartitionSpec as P

HALO = 32
LANES = 128
HALF = 64
SURF_WEIGHT = 0.02
FACE = 2.0 / 3.0
LIMIT = 32 * 1024 * 1024
ACROSS = (False, True, False, False)


def inverse(value):
    guess = pl.reciprocal(value, approx=True)
    return guess * (2.0 - value * guess)


def lane_ids(rows):
    return lax.broadcasted_iota(jnp.int32, (rows, LANES), 1)


def gather(value, select):
    high = value.astype(jnp.bfloat16)
    low = (value - high.astype(jnp.float32)).astype(jnp.bfloat16)
    return jnp.dot(jnp.concatenate([high, low], axis=1), select, preferred_element_type=jnp.float32)


def selection(lanes):
    source = lax.broadcasted_iota(jnp.int32, (LANES, LANES), 0)
    parts = [jnp.where(source == lanes[s : s + 1], 1.0, 0.0).astype(jnp.bfloat16) for s in range(4)]
    one = jnp.concatenate(parts, axis=1)
    return jnp.concatenate([one, one], axis=0)


def cut(value, s):
    return value[:, s * LANES : (s + 1) * LANES]


def row_of(position, count):
    block = lax.axis_index("normal")
    return position + block * (count - 1 - 2 * position)


def odd_surf():
    return lax.rem(lax.axis_index("surf"), 2)


def pack(plane, high):
    size = plane.shape[0] // 4
    slot = lane_ids(size) // HALO
    packed = None
    for k in range(4):
        turned = pltpu.roll(plane[k * size : (k + 1) * size], HALO * lax.rem(k + high, 4), 1)
        packed = turned if k == 0 else jnp.where(slot == k, turned, packed)
    return packed


def local_places(neighbours_ref):
    offset = lax.axis_index("surf") * LANES
    found = neighbours_ref[...]
    return found >= 0, found - offset


def spread(table, rows):
    return [jnp.broadcast_to(table[s : s + 1], (rows, LANES)) for s in range(4)]


def own_tables(neighbours_ref):
    valid, local = local_places(neighbours_ref)
    inside = valid & (local >= 0) & (local < LANES)
    return jnp.where(inside, local, -1), jnp.where(inside, SURF_WEIGHT * FACE, 0.0)


def side_tables(neighbours_ref, high):
    valid, local = local_places(neighbours_ref)
    slot = lane_ids(4) // HALO
    place = local + (HALO - high * (LANES + HALO))
    here = slot == 3 * high
    beyond = valid & here & (place >= 0) & (place < HALO)
    place = jnp.where(beyond, place, -LANES)
    weight = jnp.where(beyond, SURF_WEIGHT * FACE, 0.0)

    def repeat(value):
        value = jnp.where(here, value, 0)
        return value + pltpu.roll(value, HALO, 1) + pltpu.roll(value, 2 * HALO, 1) + pltpu.roll(value, 3 * HALO, 1)

    return repeat(place) + HALO * slot, repeat(weight)


def unpack(value, high):
    here = lane_ids(value.shape[0]) // HALO == 3 * high
    return jnp.concatenate(
        [jnp.where(here, pltpu.roll(value, HALO * lax.rem(4 - k - high, 4), 1), 0.0) for k in range(4)], axis=0
    )


def kappa_kernel(pops_hbm, absorb_hbm, emit_hbm, lines_hbm, places_hbm, walls_hbm, sources_hbm, kappa_ref, turned_ref, far_0, far_1, emit_ref, lines_ref, places_ref, walls_ref, sources_ref, pops_ref, table_ref, sems):
    rows, groups, cells = kappa_ref.shape
    levels = pops_ref.shape[0]
    pieces = 4
    step = levels // pieces
    pairs = []
    for piece in range(pieces):
        here = pl.ds(piece * step, step)
        pairs.append((pops_hbm.at[here], pops_ref.at[here]))
    pairs.append((absorb_hbm, table_ref))
    step = groups * rows // pieces
    for piece in range(pieces):
        there = pl.ds(piece * step, step)
        pairs.append((lines_hbm.at[there], lines_ref.at[there]))
    pairs += [(emit_hbm, emit_ref), (places_hbm, places_ref), (walls_hbm, walls_ref), (sources_hbm, sources_ref)]
    copies = [pltpu.make_async_copy(pair[0], pair[1], sems.at[i]) for i, pair in enumerate(pairs)]
    for copy in copies:
        copy.start()
    step = levels // pieces
    for piece in range(pieces):
        copies[piece].wait()
        here = pl.ds(piece * step, step)
        turned_ref[:, here, :] = jnp.swapaxes(pops_ref[here], 0, 1)
    copies[pieces].wait()
    table = table_ref[...]
    for pair in range(rows // 2):
        both = jnp.concatenate([turned_ref[2 * pair], turned_ref[2 * pair + 1]], axis=1)
        product = jnp.dot(table, both, preferred_element_type=jnp.float32)
        for k in range(2):
            kappa_ref[row_of(2 * pair + k, rows)] = product[:, k * cells : (k + 1) * cells]
    odd = odd_surf()
    half = groups // 2
    for r in range(rows):
        far_0[0, r] = pack(kappa_ref[r, :half], odd)
        far_1[0, r] = pack(kappa_ref[r, half:], odd)
    for copy in copies[pieces + 1 :]:
        copy.wait()
    for r in range(rows):
        far_0[1, r] = pack(lines_ref[pl.ds(row_of(r, rows), half, stride=rows), :], odd)
        far_1[1, r] = pack(lines_ref[pl.ds(half * rows + row_of(r, rows), half, stride=rows), :], odd)


def near_kernel(lines_ref, kappa_ref, neighbours_ref, current_ref, near_0, near_1, select_ref, weight_ref):
    rows, groups, cells = current_ref.shape
    half = groups // 2
    high = odd_surf()
    low_near = 1 - high
    for r in range(rows):
        current = lines_ref[pl.ds(row_of(r, rows), groups, stride=rows), :]
        current_ref[r] = current
        kappa = kappa_ref[r]
        near_0[0, r] = pack(kappa[:half], low_near)
        near_0[1, r] = pack(current[:half], low_near)
        near_1[0, r] = pack(kappa[half:], low_near)
        near_1[1, r] = pack(current[half:], low_near)
    lanes, weight = own_tables(neighbours_ref)
    select_ref[0] = selection(lanes)
    weight_ref[0] = weight
    lanes, weight = side_tables(neighbours_ref, low_near)
    select_ref[1] = selection(lanes)
    weight_ref[1] = weight
    lanes, weight = side_tables(neighbours_ref, high)
    select_ref[2] = selection(lanes)
    weight_ref[2] = weight


def own_kernel(kappa_ref, current_ref, turned_ref, emit_ref, source_ref, wall_ref, select_ref, weight_ref, base_ref, face_ref, emission_ref, rhs_ref, couple_ref):
    rows, groups, cells = kappa_ref.shape
    weight = spread(weight_ref[0], groups)
    kind = wall_ref[...]
    share = jnp.where(kind == 0, 0.5, jnp.where(kind == 1, 0.25, 0.0))
    at_wall = lax.axis_index("normal") == 0
    boundary = jnp.where(at_wall, share, 0.5)
    source = jnp.broadcast_to(source_ref[...], (groups, groups)).T * jnp.where(at_wall, share, 0.0)
    table = emit_ref[...]
    for pair in range(rows // 2):
        both = jnp.concatenate([turned_ref[2 * pair], turned_ref[2 * pair + 1]], axis=1)
        product = jnp.dot(table, both, preferred_element_type=jnp.float32)
        for k in range(2):
            emission_ref[row_of(2 * pair + k, rows)] = product[:, k * cells : (k + 1) * cells]
    emission_ref[0] = emission_ref[0] + source

    @pl.loop(0, rows // 4)
    def _(quad):
        here = pl.ds(quad * 4, 4)
        planes = jnp.concatenate([kappa_ref[here], current_ref[here]], axis=0).reshape(8 * groups, cells)
        found = gather(planes, select_ref[0])
        for k in range(4):
            r = quad * 4 + k
            kappa = kappa_ref[r]
            total = kappa + jnp.where(r == 0, boundary, 0.0) if k == 0 else kappa
            rhs = emission_ref[r]
            for s in range(4):
                couple = weight[s] * inverse(kappa + cut(found[k * groups : (k + 1) * groups], s))
                couple_ref[s, r] = couple
                total = total + couple
                rhs = rhs + couple * cut(found[(4 + k) * groups : (5 + k) * groups], s)
            base_ref[r] = total
            rhs_ref[r] = rhs
            face_ref[r] = FACE * inverse(kappa_ref[jnp.maximum(r - 1, 0)] + kappa)


def own_again_kernel(current_0, current_1, emission_ref, couple_ref, select_ref, rhs_ref):
    rows, groups, cells = emission_ref.shape

    @pl.loop(0, rows // 4)
    def _(quad):
        here = pl.ds(quad * 4, 4)
        planes = jnp.concatenate([current_0[here], current_1[here]], axis=1).reshape(4 * groups, cells)
        found = gather(planes, select_ref[0])
        for k in range(4):
            r = quad * 4 + k
            rhs = emission_ref[r]
            for s in range(4):
                rhs = rhs + couple_ref[s, r] * cut(found[k * groups : (k + 1) * groups], s)
            rhs_ref[r] = rhs


def find_sides(far, near, select_ref, found_ref):
    found_ref[0] = gather(far, select_ref[2]).reshape(found_ref.shape[1:])
    found_ref[1] = gather(near, select_ref[1]).reshape(found_ref.shape[1:])


def first_kernel(start, kappa_ref, base_ref, face_ref, rhs_ref, mine_ref, far_ref, near_mine_ref, near_ref, select_ref, weight_ref, *refs):
    couple_ref, pivot_ref, carried_ref, solved_ref, ends_ref, found_ref = refs[-6:]
    rows, groups, cells = pivot_ref.shape
    size = groups // 4
    here = pl.ds(start, groups)
    ends_ref[2] = kappa_ref[rows - 1, here]
    high = odd_surf()
    find_sides(far_ref[...].reshape(2 * rows * size, cells), near_ref[...].reshape(2 * rows * size, cells), select_ref, found_ref)
    weights = [spread(weight_ref[2], size), spread(weight_ref[1], size)]
    schur = None
    carried = None
    solved = None
    for r in range(rows):
        base = base_ref[r, here, :]
        rhs = rhs_ref[r, here, :]
        for side in range(2):
            kappa = (near_mine_ref if side else mine_ref)[0, r]
            for s in range(4):
                couple = weights[side][s] * inverse(kappa + cut(found_ref[side, r], s))
                couple_ref[side, s, r] = couple
                term = couple * cut(found_ref[side, rows + r], s)
                total = couple if s == 0 else total + couple
                terms = term if s == 0 else terms + term
            base = base + unpack(total, 1 - high if side else high)
            rhs = rhs + unpack(terms, 1 - high if side else high)
        if r == 0:
            schur = base
        else:
            schur = base + schur * carried
            rhs = rhs + face_ref[r, here, :] * solved
        if r == rows - 1:
            ends_ref[0] = schur
            ends_ref[1] = rhs
        else:
            after = face_ref[r + 1, here, :]
            pivot = inverse(schur + after)
            carried = after * pivot
            solved = rhs * pivot
            pivot_ref[r] = pivot
            carried_ref[r] = carried
            solved_ref[r] = solved


def meet_kernel(ends_ref, other_ref, carried_ref, solved_ref, current_ref, far_ref, near_ref, mix_ref):
    rows, groups, cells = current_ref.shape
    odd = odd_surf()
    face = FACE * inverse(ends_ref[2] + other_ref[2])
    own, other = ends_ref[0], other_ref[0]
    scale = inverse(own * other + face * (own + other))
    mine = (other + face) * scale
    theirs = face * scale
    mix_ref[0] = mine
    mix_ref[1] = theirs
    value = mine * ends_ref[1] + theirs * other_ref[1]
    current_ref[rows - 1] = value
    far_ref[rows - 1] = pack(value, odd)
    near_ref[rows - 1] = pack(value, 1 - odd)
    for r in range(rows - 2, -1, -1):
        value = solved_ref[r] + carried_ref[r] * value
        current_ref[r] = value
        far_ref[r] = pack(value, odd)
        near_ref[r] = pack(value, 1 - odd)


def again_kernel(start, rhs_ref, far_ref, near_ref, couple_ref, select_ref, pivot_ref, face_ref, *refs):
    solved_ref, end_ref, found_ref = refs[-3:]
    rows, groups, cells = pivot_ref.shape
    size = groups // 4
    here = pl.ds(start, groups)
    high = odd_surf()
    find_sides(far_ref[...].reshape(rows * size, cells), near_ref[...].reshape(rows * size, cells), select_ref, found_ref)
    solved = None
    for r in range(rows):
        rhs = rhs_ref[r, here, :]
        for side in range(2):
            for s in range(4):
                term = couple_ref[side, s, r] * cut(found_ref[side, r], s)
                terms = term if s == 0 else terms + term
            rhs = rhs + unpack(terms, 1 - high if side else high)
        if r > 0:
            rhs = rhs + face_ref[r, here, :] * solved
        if r == rows - 1:
            end_ref[...] = rhs
        else:
            solved = rhs * pivot_ref[r]
            solved_ref[r] = solved


def last_kernel(*refs):
    halves, (out_hbm, lines_ref, sems) = (refs[5:10], refs[:5]), refs[10:]
    copies = []
    start = 0
    for end_ref, other_ref, mix_ref, carried_ref, solved_ref in halves:
        rows, groups, cells = carried_ref.shape
        step = groups // 2
        for part in range(2):
            here = pl.ds(part * step, step)
            value = mix_ref[0, here, :] * end_ref[here, :] + mix_ref[1, here, :] * other_ref[here, :]
            lines_ref[pl.ds(start * rows + row_of(rows - 1, rows), step, stride=rows), :] = value
            for r in range(rows - 2, -1, -1):
                value = solved_ref[r, here, :] + carried_ref[r, here, :] * value
                lines_ref[pl.ds(start * rows + row_of(r, rows), step, stride=rows), :] = value
            there = pl.ds(start * rows, step * rows)
            copies.append(pltpu.make_async_copy(lines_ref.at[there], out_hbm.at[there], sems.at[len(copies)]))
            copies[-1].start()
            start = start + step
    for copy in copies:
        copy.wait()


VMEM = pl.BlockSpec(memory_space=pltpu.VMEM)
HBM = pl.BlockSpec(memory_space=pltpu.HBM)


def call(kernel, outs, *args, space=VMEM, out_space=VMEM, scratch=()):
    return pl.pallas_call(
        kernel,
        out_shape=[jax.ShapeDtypeStruct(out, jnp.float32) if isinstance(out, tuple) else out for out in outs],
        in_specs=[space] * len(args),
        out_specs=[out_space] * len(outs),
        scratch_shapes=list(scratch),
        compiler_params=pltpu.CompilerParams(vmem_limit_bytes=LIMIT),
    )(*args)


def like(value):
    return jax.ShapeDtypeStruct(value.shape, value.dtype)


def in_hbm(*values):
    return [pltpu.with_memory_space_constraint(value, pltpu.HBM) for value in values]


def far_pairs(count, across):
    pairs = []
    for block in range(2):
        for i in range(count):
            if i in (0, count - 1):
                other = count - 1 - i if across else i
                pairs.append((block * count + i, (1 - block) * count + other))
            else:
                pairs.append((block * count + i, block * count + (i + 1 if i % 2 else i - 1)))
    return pairs


def body(populations, absorb_table, emit_table, energy, wall_source, neighbours, wall_type):
    levels, rows, cells = populations.shape
    groups = absorb_table.shape[0]
    whole = (rows, groups, cells)
    plane = (groups, cells)
    side = (rows, HALO, cells)
    half = groups // 2
    half_whole = (rows, half, cells)
    half_side = (rows, HALO // 2, cells)
    found_half = pltpu.VMEM((2, rows, HALO // 2, 4 * LANES), jnp.float32)
    found_both = pltpu.VMEM((2, 2 * rows, HALO // 2, 4 * LANES), jnp.float32)
    count = lax.axis_size("surf")
    far = [far_pairs(count, across) for across in ACROSS]
    near = [(i, i ^ 1) for i in range(count)]
    swap = [(0, 1), (1, 0)]
    lines = energy.reshape(groups * rows, cells)
    places = neighbours.T
    walls = wall_type.reshape(1, cells)
    sources = wall_source.reshape(1, groups)

    kappa, turned, mine_0, mine_1, emit, lines, places, walls, sources = call(
        kappa_kernel,
        [
            whole, jax.ShapeDtypeStruct((rows, levels, cells), populations.dtype), (2,) + half_side, (2,) + half_side,
            like(emit_table), like(lines), like(places), like(walls), like(sources),
        ],
        *in_hbm(populations, absorb_table, emit_table, lines, places, walls, sources),
        space=HBM,
        scratch=[
            pltpu.VMEM(populations.shape, populations.dtype),
            pltpu.VMEM(absorb_table.shape, absorb_table.dtype),
            pltpu.SemaphoreType.DMA((13,)),
        ],
    )
    mine = (mine_0, mine_1)
    far_both = [lax.ppermute(mine[i], ("normal", "surf"), far[i]) for i in range(2)]
    current, *near_mine, select, weight = call(
        near_kernel,
        [
            whole, (2,) + half_side, (2,) + half_side,
            jax.ShapeDtypeStruct((3, 2 * LANES, 4 * LANES), jnp.bfloat16), (3, 4, LANES),
        ],
        lines, kappa, places,
    )
    near_both = [lax.ppermute(value, "surf", near) for value in near_mine]
    base, face, emission, rhs, own_couple = call(
        own_kernel, [whole, whole, whole, whole, (4,) + whole],
        kappa, current, turned, emit, sources, walls, select, weight,
    )
    firsts, others, meets = [], [], []
    for i in range(2):
        firsts.append(call(
            functools.partial(first_kernel, i * half),
            [(2, 4) + half_side, half_whole, half_whole, half_whole, (3, half, cells)],
            kappa, base, face, rhs, mine[i], far_both[i], near_mine[i], near_both[i], select, weight,
            *[done[4] for done in firsts],
            scratch=[found_both],
        ))
        others.append(lax.ppermute(firsts[i][4], "normal", swap))
    for i in range(2):
        couple, pivot, carried, solved, ends = firsts[i]
        meets.append(call(
            meet_kernel, [half_whole, half_side, half_side, (2, half, cells)], ends, others[i], carried, solved
        ))
    far_current = [lax.ppermute(meets[i][1], ("normal", "surf"), far[2 + i]) for i in range(2)]
    near_current = [lax.ppermute(meet[2], "surf", near) for meet in meets]
    (rhs,) = call(own_again_kernel, [whole], meets[0][0], meets[1][0], emission, own_couple, select)
    parts = []
    for i in range(2):
        couple, pivot, carried, solved, ends = firsts[i]
        solved, end = call(
            functools.partial(again_kernel, i * half), [half_whole, (half, cells)],
            rhs, far_current[i], near_current[i], couple, select, pivot, face, *parts[:1],
            scratch=[found_half],
        )
        parts += [end, lax.ppermute(end, "normal", swap), meets[i][3], carried, solved]
    (out,) = call(
        last_kernel, [lines.shape], *parts[5:], *parts[:5],
        out_space=HBM,
        scratch=[pltpu.VMEM(lines.shape, jnp.float32), pltpu.SemaphoreType.DMA((4,))],
    )
    return out.reshape(groups, rows, cells)


def solution(mesh):
    return jax.shard_map(
        body,
        mesh=mesh,
        in_specs=(
            P(None, "normal", "surf"),
            P(),
            P(),
            P(None, "normal", "surf"),
            P(),
            P("surf", None),
            P("surf"),
        ),
        out_specs=P(None, "normal", "surf"),
        check_vma=False,
    )
```

```python
import functools

import jax
import jax.numpy as jnp
from jax import lax
from jax.experimental import pallas as pl
from jax.experimental.pallas import tpu as pltpu
from jax.sharding import PartitionSpec as P

HALO = 32
LANES = 128
HALF = 64
SURF_WEIGHT = 0.02
FACE = 2.0 / 3.0
LIMIT = 32 * 1024 * 1024
ACROSS = (False, True, False, False)


def inverse(value):
    guess = pl.reciprocal(value, approx=True)
    return guess * (2.0 - value * guess)


def lane_ids(rows):
    return lax.broadcasted_iota(jnp.int32, (rows, LANES), 1)


def gather(value, select):
    high = value.astype(jnp.bfloat16)
    low = (value - high.astype(jnp.float32)).astype(jnp.bfloat16)
    return jnp.dot(jnp.concatenate([high, low], axis=1), select, preferred_element_type=jnp.float32)


def selection(lanes):
    source = lax.broadcasted_iota(jnp.int32, (LANES, LANES), 0)
    parts = [jnp.where(source == lanes[s : s + 1], 1.0, 0.0).astype(jnp.bfloat16) for s in range(4)]
    one = jnp.concatenate(parts, axis=1)
    return jnp.concatenate([one, one], axis=0)


def cut(value, s):
    return value[:, s * LANES : (s + 1) * LANES]


def row_of(position, count):
    block = lax.axis_index("normal")
    return position + block * (count - 1 - 2 * position)


def odd_surf():
    return lax.rem(lax.axis_index("surf"), 2)


def pack(plane, high):
    size = plane.shape[0] // 4
    slot = lane_ids(size) // HALO
    packed = None
    for k in range(4):
        turned = pltpu.roll(plane[k * size : (k + 1) * size], HALO * lax.rem(k + high, 4), 1)
        packed = turned if k == 0 else jnp.where(slot == k, turned, packed)
    return packed


def local_places(neighbours_ref):
    offset = lax.axis_index("surf") * LANES
    found = neighbours_ref[...]
    return found >= 0, found - offset


def spread(table, rows):
    return [jnp.broadcast_to(table[s : s + 1], (rows, LANES)) for s in range(4)]


def own_tables(neighbours_ref):
    valid, local = local_places(neighbours_ref)
    inside = valid & (local >= 0) & (local < LANES)
    return jnp.where(inside, local, -1), jnp.where(inside, SURF_WEIGHT * FACE, 0.0)


def side_tables(neighbours_ref, high):
    valid, local = local_places(neighbours_ref)
    slot = lane_ids(4) // HALO
    place = local + (HALO - high * (LANES + HALO))
    here = slot == 3 * high
    beyond = valid & here & (place >= 0) & (place < HALO)
    place = jnp.where(beyond, place, -LANES)
    weight = jnp.where(beyond, SURF_WEIGHT * FACE, 0.0)

    def repeat(value):
        value = jnp.where(here, value, 0)
        return value + pltpu.roll(value, HALO, 1) + pltpu.roll(value, 2 * HALO, 1) + pltpu.roll(value, 3 * HALO, 1)

    return repeat(place) + HALO * slot, repeat(weight)


def unpack(value, high):
    here = lane_ids(value.shape[0]) // HALO == 3 * high
    return jnp.concatenate(
        [jnp.where(here, pltpu.roll(value, HALO * lax.rem(4 - k - high, 4), 1), 0.0) for k in range(4)], axis=0
    )


def kappa_kernel(pops_hbm, absorb_hbm, emit_hbm, lines_hbm, places_hbm, walls_hbm, sources_hbm, kappa_ref, turned_ref, far_0, emit_ref, lines_ref, places_ref, walls_ref, sources_ref, pops_ref, table_ref, sems):
    rows, groups, cells = kappa_ref.shape
    levels = pops_ref.shape[0]
    pieces = 4
    step = levels // pieces
    pairs = []
    for piece in range(pieces):
        here = pl.ds(piece * step, step)
        pairs.append((pops_hbm.at[here], pops_ref.at[here]))
    pairs.append((absorb_hbm, table_ref))
    step = groups * rows // pieces
    for piece in range(pieces):
        there = pl.ds(piece * step, step)
        pairs.append((lines_hbm.at[there], lines_ref.at[there]))
    pairs += [(emit_hbm, emit_ref), (places_hbm, places_ref), (walls_hbm, walls_ref), (sources_hbm, sources_ref)]
    copies = [pltpu.make_async_copy(pair[0], pair[1], sems.at[i]) for i, pair in enumerate(pairs)]
    for copy in copies:
        copy.start()
    step = levels // pieces
    for piece in range(pieces):
        copies[piece].wait()
        here = pl.ds(piece * step, step)
        turned_ref[:, here, :] = jnp.swapaxes(pops_ref[here], 0, 1)
    copies[pieces].wait()
    table = table_ref[...]
    for pair in range(rows // 2):
        both = jnp.concatenate([turned_ref[2 * pair], turned_ref[2 * pair + 1]], axis=1)
        product = jnp.dot(table, both, preferred_element_type=jnp.float32)
        for k in range(2):
            kappa_ref[row_of(2 * pair + k, rows)] = product[:, k * cells : (k + 1) * cells]
    odd = odd_surf()
    half = groups // 2
    for r in range(rows):
        far_0[0, r] = pack(kappa_ref[r, :half], odd)
    for copy in copies[pieces + 1 :]:
        copy.wait()
    for r in range(rows):
        far_0[1, r] = pack(lines_ref[pl.ds(row_of(r, rows), half, stride=rows), :], odd)


def near_kernel(lines_ref, kappa_ref, neighbours_ref, current_ref, far_1, near_0, near_1, select_ref, weight_ref):
    rows, groups, cells = current_ref.shape
    half = groups // 2
    high = odd_surf()
    low_near = 1 - high
    for r in range(rows):
        current = lines_ref[pl.ds(row_of(r, rows), groups, stride=rows), :]
        current_ref[r] = current
        kappa = kappa_ref[r]
        far_1[0, r] = pack(kappa[half:], high)
        far_1[1, r] = pack(current[half:], high)
        near_0[0, r] = pack(kappa[:half], low_near)
        near_0[1, r] = pack(current[:half], low_near)
        near_1[0, r] = pack(kappa[half:], low_near)
        near_1[1, r] = pack(current[half:], low_near)
    lanes, weight = own_tables(neighbours_ref)
    select_ref[0] = selection(lanes)
    weight_ref[0] = weight
    lanes, weight = side_tables(neighbours_ref, low_near)
    select_ref[1] = selection(lanes)
    weight_ref[1] = weight
    lanes, weight = side_tables(neighbours_ref, high)
    select_ref[2] = selection(lanes)
    weight_ref[2] = weight


def own_kernel(kappa_ref, current_ref, turned_ref, emit_ref, source_ref, wall_ref, select_ref, weight_ref, base_ref, face_ref, emission_ref, rhs_ref, couple_ref):
    rows, groups, cells = kappa_ref.shape
    weight = spread(weight_ref[0], groups)
    kind = wall_ref[...]
    share = jnp.where(kind == 0, 0.5, jnp.where(kind == 1, 0.25, 0.0))
    at_wall = lax.axis_index("normal") == 0
    boundary = jnp.where(at_wall, share, 0.5)
    source = jnp.broadcast_to(source_ref[...], (groups, groups)).T * jnp.where(at_wall, share, 0.0)
    table = emit_ref[...]
    for pair in range(rows // 2):
        both = jnp.concatenate([turned_ref[2 * pair], turned_ref[2 * pair + 1]], axis=1)
        product = jnp.dot(table, both, preferred_element_type=jnp.float32)
        for k in range(2):
            emission_ref[row_of(2 * pair + k, rows)] = product[:, k * cells : (k + 1) * cells]
    emission_ref[0] = emission_ref[0] + source

    @pl.loop(0, rows // 4)
    def _(quad):
        here = pl.ds(quad * 4, 4)
        planes = jnp.concatenate([kappa_ref[here], current_ref[here]], axis=0).reshape(8 * groups, cells)
        found = gather(planes, select_ref[0])
        for k in range(4):
            r = quad * 4 + k
            kappa = kappa_ref[r]
            total = kappa + jnp.where(r == 0, boundary, 0.0) if k == 0 else kappa
            rhs = emission_ref[r]
            for s in range(4):
                couple = weight[s] * inverse(kappa + cut(found[k * groups : (k + 1) * groups], s))
                couple_ref[s, r] = couple
                total = total + couple
                rhs = rhs + couple * cut(found[(4 + k) * groups : (5 + k) * groups], s)
            base_ref[r] = total
            rhs_ref[r] = rhs
            face_ref[r] = FACE * inverse(kappa_ref[jnp.maximum(r - 1, 0)] + kappa)


def own_again_kernel(current_0, current_1, emission_ref, couple_ref, select_ref, rhs_ref):
    rows, groups, cells = emission_ref.shape

    @pl.loop(0, rows // 4)
    def _(quad):
        here = pl.ds(quad * 4, 4)
        planes = jnp.concatenate([current_0[here], current_1[here]], axis=1).reshape(4 * groups, cells)
        found = gather(planes, select_ref[0])
        for k in range(4):
            r = quad * 4 + k
            rhs = emission_ref[r]
            for s in range(4):
                rhs = rhs + couple_ref[s, r] * cut(found[k * groups : (k + 1) * groups], s)
            rhs_ref[r] = rhs


def find_sides(far, near, select_ref, found_ref):
    found_ref[0] = gather(far, select_ref[2]).reshape(found_ref.shape[1:])
    found_ref[1] = gather(near, select_ref[1]).reshape(found_ref.shape[1:])


def first_kernel(start, kappa_ref, base_ref, face_ref, rhs_ref, mine_ref, far_ref, near_mine_ref, near_ref, select_ref, weight_ref, *refs):
    couple_ref, pivot_ref, carried_ref, solved_ref, ends_ref, found_ref = refs[-6:]
    rows, groups, cells = pivot_ref.shape
    size = groups // 4
    here = pl.ds(start, groups)
    ends_ref[2] = kappa_ref[rows - 1, here]
    high = odd_surf()
    find_sides(far_ref[...].reshape(2 * rows * size, cells), near_ref[...].reshape(2 * rows * size, cells), select_ref, found_ref)
    weights = [spread(weight_ref[2], size), spread(weight_ref[1], size)]
    schur = None
    carried = None
    solved = None
    for r in range(rows):
        base = base_ref[r, here, :]
        rhs = rhs_ref[r, here, :]
        for side in range(2):
            kappa = (near_mine_ref if side else mine_ref)[0, r]
            for s in range(4):
                couple = weights[side][s] * inverse(kappa + cut(found_ref[side, r], s))
                couple_ref[side, s, r] = couple
                term = couple * cut(found_ref[side, rows + r], s)
                total = couple if s == 0 else total + couple
                terms = term if s == 0 else terms + term
            base = base + unpack(total, 1 - high if side else high)
            rhs = rhs + unpack(terms, 1 - high if side else high)
        if r == 0:
            schur = base
        else:
            schur = base + schur * carried
            rhs = rhs + face_ref[r, here, :] * solved
        if r == rows - 1:
            ends_ref[0] = schur
            ends_ref[1] = rhs
        else:
            after = face_ref[r + 1, here, :]
            pivot = inverse(schur + after)
            carried = after * pivot
            solved = rhs * pivot
            pivot_ref[r] = pivot
            carried_ref[r] = carried
            solved_ref[r] = solved


def meet_kernel(ends_ref, other_ref, carried_ref, solved_ref, current_ref, far_ref, near_ref, mix_ref):
    rows, groups, cells = current_ref.shape
    odd = odd_surf()
    face = FACE * inverse(ends_ref[2] + other_ref[2])
    own, other = ends_ref[0], other_ref[0]
    scale = inverse(own * other + face * (own + other))
    mine = (other + face) * scale
    theirs = face * scale
    mix_ref[0] = mine
    mix_ref[1] = theirs
    value = mine * ends_ref[1] + theirs * other_ref[1]
    current_ref[rows - 1] = value
    far_ref[rows - 1] = pack(value, odd)
    near_ref[rows - 1] = pack(value, 1 - odd)
    for r in range(rows - 2, -1, -1):
        value = solved_ref[r] + carried_ref[r] * value
        current_ref[r] = value
        far_ref[r] = pack(value, odd)
        near_ref[r] = pack(value, 1 - odd)


def again_kernel(start, rhs_ref, far_ref, near_ref, couple_ref, select_ref, pivot_ref, face_ref, *refs):
    solved_ref, end_ref, found_ref = refs[-3:]
    if len(refs) > 3:
        end_ref[0] = refs[0][...]
        end_ref = end_ref.at[1]
    rows, groups, cells = pivot_ref.shape
    size = groups // 4
    here = pl.ds(start, groups)
    high = odd_surf()
    find_sides(far_ref[...].reshape(rows * size, cells), near_ref[...].reshape(rows * size, cells), select_ref, found_ref)
    solved = None
    for r in range(rows):
        rhs = rhs_ref[r, here, :]
        for side in range(2):
            for s in range(4):
                term = couple_ref[side, s, r] * cut(found_ref[side, r], s)
                terms = term if s == 0 else terms + term
            rhs = rhs + unpack(terms, 1 - high if side else high)
        if r > 0:
            rhs = rhs + face_ref[r, here, :] * solved
        if r == rows - 1:
            end_ref[...] = rhs
        else:
            solved = rhs * pivot_ref[r]
            solved_ref[r] = solved


def last_kernel(*refs):
    ends_ref, others_ref, *halves, out_hbm, lines_ref, sems = refs
    copies = []
    start = 0
    for i in range(2):
        mix_ref, carried_ref, solved_ref = halves[3 * i : 3 * i + 3]
        end_ref, other_ref = ends_ref.at[i], others_ref.at[i]
        rows, groups, cells = carried_ref.shape
        step = groups // 2
        for part in range(2):
            here = pl.ds(part * step, step)
            value = mix_ref[0, here, :] * end_ref[here, :] + mix_ref[1, here, :] * other_ref[here, :]
            lines_ref[pl.ds(start * rows + row_of(rows - 1, rows), step, stride=rows), :] = value
            for r in range(rows - 2, -1, -1):
                value = solved_ref[r, here, :] + carried_ref[r, here, :] * value
                lines_ref[pl.ds(start * rows + row_of(r, rows), step, stride=rows), :] = value
            there = pl.ds(start * rows, step * rows)
            copies.append(pltpu.make_async_copy(lines_ref.at[there], out_hbm.at[there], sems.at[len(copies)]))
            copies[-1].start()
            start = start + step
    for copy in copies:
        copy.wait()


VMEM = pl.BlockSpec(memory_space=pltpu.VMEM)
HBM = pl.BlockSpec(memory_space=pltpu.HBM)


def call(kernel, outs, *args, space=VMEM, out_space=VMEM, scratch=()):
    return pl.pallas_call(
        kernel,
        out_shape=[jax.ShapeDtypeStruct(out, jnp.float32) if isinstance(out, tuple) else out for out in outs],
        in_specs=[space] * len(args),
        out_specs=[out_space] * len(outs),
        scratch_shapes=list(scratch),
        compiler_params=pltpu.CompilerParams(vmem_limit_bytes=LIMIT),
    )(*args)


def like(value):
    return jax.ShapeDtypeStruct(value.shape, value.dtype)


def in_hbm(*values):
    return [pltpu.with_memory_space_constraint(value, pltpu.HBM) for value in values]


def far_pairs(count, across):
    pairs = []
    for block in range(2):
        for i in range(count):
            if i in (0, count - 1):
                other = count - 1 - i if across else i
                pairs.append((block * count + i, (1 - block) * count + other))
            else:
                pairs.append((block * count + i, block * count + (i + 1 if i % 2 else i - 1)))
    return pairs


def body(populations, absorb_table, emit_table, energy, wall_source, neighbours, wall_type):
    levels, rows, cells = populations.shape
    groups = absorb_table.shape[0]
    whole = (rows, groups, cells)
    plane = (groups, cells)
    side = (rows, HALO, cells)
    half = groups // 2
    half_whole = (rows, half, cells)
    half_side = (rows, HALO // 2, cells)
    found_half = pltpu.VMEM((2, rows, HALO // 2, 4 * LANES), jnp.float32)
    found_both = pltpu.VMEM((2, 2 * rows, HALO // 2, 4 * LANES), jnp.float32)
    count = lax.axis_size("surf")
    far = [far_pairs(count, across) for across in ACROSS]
    near = [(i, i ^ 1) for i in range(count)]
    swap = [(0, 1), (1, 0)]
    lines = energy.reshape(groups * rows, cells)
    places = neighbours.T
    walls = wall_type.reshape(1, cells)
    sources = wall_source.reshape(1, groups)

    kappa, turned, mine_0, emit, lines, places, walls, sources = call(
        kappa_kernel,
        [
            whole, jax.ShapeDtypeStruct((rows, levels, cells), populations.dtype), (2,) + half_side,
            like(emit_table), like(lines), like(places), like(walls), like(sources),
        ],
        *in_hbm(populations, absorb_table, emit_table, lines, places, walls, sources),
        space=HBM,
        scratch=[
            pltpu.VMEM(populations.shape, populations.dtype),
            pltpu.VMEM(absorb_table.shape, absorb_table.dtype),
            pltpu.SemaphoreType.DMA((13,)),
        ],
    )
    far_0 = lax.ppermute(mine_0, ("normal", "surf"), far[0])
    current, mine_1, *near_mine, select, weight = call(
        near_kernel,
        [
            whole, (2,) + half_side, (2,) + half_side, (2,) + half_side,
            jax.ShapeDtypeStruct((3, 2 * LANES, 4 * LANES), jnp.bfloat16), (3, 4, LANES),
        ],
        lines, kappa, places,
    )
    mine = (mine_0, mine_1)
    far_both = (far_0, lax.ppermute(mine_1, ("normal", "surf"), far[1]))
    near_both = [lax.ppermute(value, "surf", near) for value in near_mine]
    base, face, emission, rhs, own_couple = call(
        own_kernel, [whole, whole, whole, whole, (4,) + whole],
        kappa, current, turned, emit, sources, walls, select, weight,
    )
    firsts, others, meets = [], [], []
    for i in range(2):
        firsts.append(call(
            functools.partial(first_kernel, i * half),
            [(2, 4) + half_side, half_whole, half_whole, half_whole, (3, half, cells)],
            kappa, base, face, rhs, mine[i], far_both[i], near_mine[i], near_both[i], select, weight,
            *[done[4] for done in firsts],
            scratch=[found_both],
        ))
        others.append(lax.ppermute(firsts[i][4], "normal", swap))
    for i in range(2):
        couple, pivot, carried, solved, ends = firsts[i]
        meets.append(call(
            meet_kernel, [half_whole, half_side, half_side, (2, half, cells)], ends, others[i], carried, solved
        ))
    far_current = [lax.ppermute(meets[i][1], ("normal", "surf"), far[2 + i]) for i in range(2)]
    near_current = [lax.ppermute(meet[2], "surf", near) for meet in meets]
    (rhs,) = call(own_again_kernel, [whole], meets[0][0], meets[1][0], emission, own_couple, select)
    parts = []
    for i in range(2):
        couple, pivot, carried, solved, ends = firsts[i]
        solved, end = call(
            functools.partial(again_kernel, i * half), [half_whole, (2, half, cells) if i else (half, cells)],
            rhs, far_current[i], near_current[i], couple, select, pivot, face, *parts[:1],
            scratch=[found_half],
        )
        parts += [end, meets[i][3], carried, solved]
    other_ends = lax.ppermute(end, "normal", swap)
    (out,) = call(
        last_kernel, [lines.shape], end, other_ends, *parts[1:4], *parts[5:],
        out_space=HBM,
        scratch=[pltpu.VMEM(lines.shape, jnp.float32), pltpu.SemaphoreType.DMA((4,))],
    )
    return out.reshape(groups, rows, cells)


def solution(mesh):
    return jax.shard_map(
        body,
        mesh=mesh,
        in_specs=(
            P(None, "normal", "surf"),
            P(),
            P(),
            P(None, "normal", "surf"),
            P(),
            P("surf", None),
            P("surf"),
        ),
        out_specs=P(None, "normal", "surf"),
        check_vma=False,
    )
```

```python
import functools

import jax
import jax.numpy as jnp
from jax import lax
from jax.experimental import pallas as pl
from jax.experimental.pallas import tpu as pltpu
from jax.sharding import PartitionSpec as P

HALO = 32
LANES = 128
HALF = 64
SURF_WEIGHT = 0.02
FACE = 2.0 / 3.0
LIMIT = 32 * 1024 * 1024
ACROSS = (False, True, False, False)


def inverse(value):
    guess = pl.reciprocal(value, approx=True)
    return guess * (2.0 - value * guess)


def lane_ids(rows):
    return lax.broadcasted_iota(jnp.int32, (rows, LANES), 1)


def gather(value, select):
    high = value.astype(jnp.bfloat16)
    low = (value - high.astype(jnp.float32)).astype(jnp.bfloat16)
    return jnp.dot(jnp.concatenate([high, low], axis=1), select, preferred_element_type=jnp.float32)


def selection(lanes):
    source = lax.broadcasted_iota(jnp.int32, (LANES, LANES), 0)
    parts = [jnp.where(source == lanes[s : s + 1], 1.0, 0.0).astype(jnp.bfloat16) for s in range(4)]
    one = jnp.concatenate(parts, axis=1)
    return jnp.concatenate([one, one], axis=0)


def cut(value, s):
    return value[:, s * LANES : (s + 1) * LANES]


def row_of(position, count):
    block = lax.axis_index("normal")
    return position + block * (count - 1 - 2 * position)


def odd_surf():
    return lax.rem(lax.axis_index("surf"), 2)


def pack(plane, high):
    size = plane.shape[0] // 4
    slot = lane_ids(size) // HALO
    packed = None
    for k in range(4):
        turned = pltpu.roll(plane[k * size : (k + 1) * size], HALO * lax.rem(k + high, 4), 1)
        packed = turned if k == 0 else jnp.where(slot == k, turned, packed)
    return packed


def local_places(neighbours_ref):
    offset = lax.axis_index("surf") * LANES
    found = neighbours_ref[...]
    return found >= 0, found - offset


def spread(table, rows):
    return [jnp.broadcast_to(table[s : s + 1], (rows, LANES)) for s in range(4)]


def own_tables(neighbours_ref):
    valid, local = local_places(neighbours_ref)
    inside = valid & (local >= 0) & (local < LANES)
    return jnp.where(inside, local, -1), jnp.where(inside, SURF_WEIGHT * FACE, 0.0)


def side_tables(neighbours_ref, high):
    valid, local = local_places(neighbours_ref)
    slot = lane_ids(4) // HALO
    place = local + (HALO - high * (LANES + HALO))
    here = slot == 3 * high
    beyond = valid & here & (place >= 0) & (place < HALO)
    place = jnp.where(beyond, place, -LANES)
    weight = jnp.where(beyond, SURF_WEIGHT * FACE, 0.0)

    def repeat(value):
        value = jnp.where(here, value, 0)
        return value + pltpu.roll(value, HALO, 1) + pltpu.roll(value, 2 * HALO, 1) + pltpu.roll(value, 3 * HALO, 1)

    return repeat(place) + HALO * slot, repeat(weight)


def unpack(value, high):
    here = lane_ids(value.shape[0]) // HALO == 3 * high
    return jnp.concatenate(
        [jnp.where(here, pltpu.roll(value, HALO * lax.rem(4 - k - high, 4), 1), 0.0) for k in range(4)], axis=0
    )


def kappa_kernel(pops_hbm, absorb_hbm, emit_hbm, lines_hbm, places_hbm, walls_hbm, sources_hbm, kappa_ref, turned_ref, far_0, emit_ref, lines_ref, places_ref, walls_ref, sources_ref, pops_ref, table_ref, sems):
    rows, groups, cells = kappa_ref.shape
    levels = pops_ref.shape[0]
    pieces = 4
    step = levels // pieces
    pairs = []
    for piece in range(pieces):
        here = pl.ds(piece * step, step)
        pairs.append((pops_hbm.at[here], pops_ref.at[here]))
    pairs.append((absorb_hbm, table_ref))
    step = groups * rows // pieces
    for piece in range(pieces):
        there = pl.ds(piece * step, step)
        pairs.append((lines_hbm.at[there], lines_ref.at[there]))
    pairs += [(emit_hbm, emit_ref), (places_hbm, places_ref), (walls_hbm, walls_ref), (sources_hbm, sources_ref)]
    copies = [pltpu.make_async_copy(pair[0], pair[1], sems.at[i]) for i, pair in enumerate(pairs)]
    for copy in copies:
        copy.start()
    step = levels // pieces
    for piece in range(pieces):
        copies[piece].wait()
        here = pl.ds(piece * step, step)
        turned_ref[:, here, :] = jnp.swapaxes(pops_ref[here], 0, 1)
    copies[pieces].wait()
    table = table_ref[...]
    for pair in range(rows // 2):
        both = jnp.concatenate([turned_ref[2 * pair], turned_ref[2 * pair + 1]], axis=1)
        product = jnp.dot(table, both, preferred_element_type=jnp.float32)
        for k in range(2):
            kappa_ref[row_of(2 * pair + k, rows)] = product[:, k * cells : (k + 1) * cells]
    odd = odd_surf()
    half = groups // 2
    for r in range(rows):
        far_0[0, r] = pack(kappa_ref[r, :half], odd)
    for copy in copies[pieces + 1 :]:
        copy.wait()
    for r in range(rows):
        far_0[1, r] = pack(lines_ref[pl.ds(row_of(r, rows), half, stride=rows), :], odd)


def near_kernel(lines_ref, kappa_ref, neighbours_ref, current_ref, far_1, near_0, near_1, select_ref, weight_ref):
    rows, groups, cells = current_ref.shape
    half = groups // 2
    high = odd_surf()
    low_near = 1 - high
    for r in range(rows):
        current = lines_ref[pl.ds(row_of(r, rows), groups, stride=rows), :]
        current_ref[r] = current
        kappa = kappa_ref[r]
        far_1[0, r] = pack(kappa[half:], high)
        far_1[1, r] = pack(current[half:], high)
        near_0[0, r] = pack(kappa[:half], low_near)
        near_0[1, r] = pack(current[:half], low_near)
        near_1[0, r] = pack(kappa[half:], low_near)
        near_1[1, r] = pack(current[half:], low_near)
    lanes, weight = own_tables(neighbours_ref)
    select_ref[0] = selection(lanes)
    weight_ref[0] = weight
    lanes, weight = side_tables(neighbours_ref, low_near)
    select_ref[1] = selection(lanes)
    weight_ref[1] = weight
    lanes, weight = side_tables(neighbours_ref, high)
    select_ref[2] = selection(lanes)
    weight_ref[2] = weight


def own_kernel(kappa_ref, current_ref, turned_ref, emit_ref, source_ref, wall_ref, select_ref, weight_ref, base_ref, face_ref, emission_ref, rhs_ref, couple_ref):
    rows, groups, cells = kappa_ref.shape
    weight = spread(weight_ref[0], groups)
    kind = wall_ref[...]
    share = jnp.where(kind == 0, 0.5, jnp.where(kind == 1, 0.25, 0.0))
    at_wall = lax.axis_index("normal") == 0
    boundary = jnp.where(at_wall, share, 0.5)
    source = jnp.broadcast_to(source_ref[...], (groups, groups)).T * jnp.where(at_wall, share, 0.0)
    table = emit_ref[...]
    for pair in range(rows // 2):
        both = jnp.concatenate([turned_ref[2 * pair], turned_ref[2 * pair + 1]], axis=1)
        product = jnp.dot(table, both, preferred_element_type=jnp.float32)
        for k in range(2):
            emission_ref[row_of(2 * pair + k, rows)] = product[:, k * cells : (k + 1) * cells]
    emission_ref[0] = emission_ref[0] + source

    @pl.loop(0, rows // 4)
    def _(quad):
        here = pl.ds(quad * 4, 4)
        planes = jnp.concatenate([kappa_ref[here], current_ref[here]], axis=0).reshape(8 * groups, cells)
        found = gather(planes, select_ref[0])
        for k in range(4):
            r = quad * 4 + k
            kappa = kappa_ref[r]
            total = kappa + jnp.where(r == 0, boundary, 0.0) if k == 0 else kappa
            rhs = emission_ref[r]
            for s in range(4):
                couple = weight[s] * inverse(kappa + cut(found[k * groups : (k + 1) * groups], s))
                couple_ref[s, r] = couple
                total = total + couple
                rhs = rhs + couple * cut(found[(4 + k) * groups : (5 + k) * groups], s)
            base_ref[r] = total
            rhs_ref[r] = rhs
            face_ref[r] = FACE * inverse(kappa_ref[jnp.maximum(r - 1, 0)] + kappa)


def own_again_kernel(current_0, current_1, emission_ref, couple_ref, select_ref, rhs_ref):
    rows, groups, cells = emission_ref.shape

    @pl.loop(0, rows // 4)
    def _(quad):
        here = pl.ds(quad * 4, 4)
        planes = jnp.concatenate([current_0[here], current_1[here]], axis=1).reshape(4 * groups, cells)
        found = gather(planes, select_ref[0])
        for k in range(4):
            r = quad * 4 + k
            rhs = emission_ref[r]
            for s in range(4):
                rhs = rhs + couple_ref[s, r] * cut(found[k * groups : (k + 1) * groups], s)
            rhs_ref[r] = rhs


def find_sides(far, near, select_ref, found_ref):
    found_ref[0] = gather(far, select_ref[2]).reshape(found_ref.shape[1:])
    found_ref[1] = gather(near, select_ref[1]).reshape(found_ref.shape[1:])


def first_kernel(start, kappa_ref, base_ref, face_ref, rhs_ref, mine_ref, far_ref, near_mine_ref, near_ref, select_ref, weight_ref, *refs):
    couple_ref, pivot_ref, carried_ref, solved_ref, ends_ref, found_ref = refs[-6:]
    rows, groups, cells = pivot_ref.shape
    size = groups // 4
    here = pl.ds(start, groups)
    if start == 0:
        ends_ref[2] = kappa_ref[rows - 1, here]
        ends_ref[3] = kappa_ref[rows - 1, pl.ds(groups, groups)]
    high = odd_surf()
    find_sides(far_ref[...].reshape(2 * rows * size, cells), near_ref[...].reshape(2 * rows * size, cells), select_ref, found_ref)
    weights = [spread(weight_ref[2], size), spread(weight_ref[1], size)]
    schur = None
    carried = None
    solved = None
    for r in range(rows):
        base = base_ref[r, here, :]
        rhs = rhs_ref[r, here, :]
        for side in range(2):
            kappa = (near_mine_ref if side else mine_ref)[0, r]
            for s in range(4):
                couple = weights[side][s] * inverse(kappa + cut(found_ref[side, r], s))
                couple_ref[side, s, r] = couple
                term = couple * cut(found_ref[side, rows + r], s)
                total = couple if s == 0 else total + couple
                terms = term if s == 0 else terms + term
            base = base + unpack(total, 1 - high if side else high)
            rhs = rhs + unpack(terms, 1 - high if side else high)
        if r == 0:
            schur = base
        else:
            schur = base + schur * carried
            rhs = rhs + face_ref[r, here, :] * solved
        if r == rows - 1:
            ends_ref[0] = schur
            ends_ref[1] = rhs
        else:
            after = face_ref[r + 1, here, :]
            pivot = inverse(schur + after)
            carried = after * pivot
            solved = rhs * pivot
            pivot_ref[r] = pivot
            carried_ref[r] = carried
            solved_ref[r] = solved


def meet_kernel(edge, ends_ref, other_ref, edges_ref, other_edges_ref, carried_ref, solved_ref, current_ref, far_ref, near_ref, mix_ref):
    rows, groups, cells = current_ref.shape
    odd = odd_surf()
    face = FACE * inverse(edges_ref[edge] + other_edges_ref[edge])
    own, other = ends_ref[0], other_ref[0]
    scale = inverse(own * other + face * (own + other))
    mine = (other + face) * scale
    theirs = face * scale
    mix_ref[0] = mine
    mix_ref[1] = theirs
    value = mine * ends_ref[1] + theirs * other_ref[1]
    current_ref[rows - 1] = value
    far_ref[rows - 1] = pack(value, odd)
    near_ref[rows - 1] = pack(value, 1 - odd)
    for r in range(rows - 2, -1, -1):
        value = solved_ref[r] + carried_ref[r] * value
        current_ref[r] = value
        far_ref[r] = pack(value, odd)
        near_ref[r] = pack(value, 1 - odd)


def again_kernel(start, rhs_ref, far_ref, near_ref, couple_ref, select_ref, pivot_ref, face_ref, *refs):
    solved_ref, end_ref, found_ref = refs[-3:]
    if len(refs) > 3:
        end_ref[0] = refs[0][...]
        end_ref = end_ref.at[1]
    rows, groups, cells = pivot_ref.shape
    size = groups // 4
    here = pl.ds(start, groups)
    high = odd_surf()
    find_sides(far_ref[...].reshape(rows * size, cells), near_ref[...].reshape(rows * size, cells), select_ref, found_ref)
    solved = None
    for r in range(rows):
        rhs = rhs_ref[r, here, :]
        for side in range(2):
            for s in range(4):
                term = couple_ref[side, s, r] * cut(found_ref[side, r], s)
                terms = term if s == 0 else terms + term
            rhs = rhs + unpack(terms, 1 - high if side else high)
        if r > 0:
            rhs = rhs + face_ref[r, here, :] * solved
        if r == rows - 1:
            end_ref[...] = rhs
        else:
            solved = rhs * pivot_ref[r]
            solved_ref[r] = solved


def last_kernel(*refs):
    ends_ref, others_ref, *halves, out_hbm, lines_ref, sems = refs
    copies = []
    start = 0
    for i in range(2):
        mix_ref, carried_ref, solved_ref = halves[3 * i : 3 * i + 3]
        end_ref, other_ref = ends_ref.at[i], others_ref.at[i]
        rows, groups, cells = carried_ref.shape
        step = groups // 2
        for part in range(2):
            here = pl.ds(part * step, step)
            value = mix_ref[0, here, :] * end_ref[here, :] + mix_ref[1, here, :] * other_ref[here, :]
            lines_ref[pl.ds(start * rows + row_of(rows - 1, rows), step, stride=rows), :] = value
            for r in range(rows - 2, -1, -1):
                value = solved_ref[r, here, :] + carried_ref[r, here, :] * value
                lines_ref[pl.ds(start * rows + row_of(r, rows), step, stride=rows), :] = value
            there = pl.ds(start * rows, step * rows)
            copies.append(pltpu.make_async_copy(lines_ref.at[there], out_hbm.at[there], sems.at[len(copies)]))
            copies[-1].start()
            start = start + step
    for copy in copies:
        copy.wait()


VMEM = pl.BlockSpec(memory_space=pltpu.VMEM)
HBM = pl.BlockSpec(memory_space=pltpu.HBM)


def call(kernel, outs, *args, space=VMEM, out_space=VMEM, scratch=()):
    return pl.pallas_call(
        kernel,
        out_shape=[jax.ShapeDtypeStruct(out, jnp.float32) if isinstance(out, tuple) else out for out in outs],
        in_specs=[space] * len(args),
        out_specs=[out_space] * len(outs),
        scratch_shapes=list(scratch),
        compiler_params=pltpu.CompilerParams(vmem_limit_bytes=LIMIT),
    )(*args)


def like(value):
    return jax.ShapeDtypeStruct(value.shape, value.dtype)


def in_hbm(*values):
    return [pltpu.with_memory_space_constraint(value, pltpu.HBM) for value in values]


def far_pairs(count, across):
    pairs = []
    for block in range(2):
        for i in range(count):
            if i in (0, count - 1):
                other = count - 1 - i if across else i
                pairs.append((block * count + i, (1 - block) * count + other))
            else:
                pairs.append((block * count + i, block * count + (i + 1 if i % 2 else i - 1)))
    return pairs


def body(populations, absorb_table, emit_table, energy, wall_source, neighbours, wall_type):
    levels, rows, cells = populations.shape
    groups = absorb_table.shape[0]
    whole = (rows, groups, cells)
    plane = (groups, cells)
    side = (rows, HALO, cells)
    half = groups // 2
    half_whole = (rows, half, cells)
    half_side = (rows, HALO // 2, cells)
    found_half = pltpu.VMEM((2, rows, HALO // 2, 4 * LANES), jnp.float32)
    found_both = pltpu.VMEM((2, 2 * rows, HALO // 2, 4 * LANES), jnp.float32)
    count = lax.axis_size("surf")
    far = [far_pairs(count, across) for across in ACROSS]
    near = [(i, i ^ 1) for i in range(count)]
    swap = [(0, 1), (1, 0)]
    lines = energy.reshape(groups * rows, cells)
    places = neighbours.T
    walls = wall_type.reshape(1, cells)
    sources = wall_source.reshape(1, groups)

    kappa, turned, mine_0, emit, lines, places, walls, sources = call(
        kappa_kernel,
        [
            whole, jax.ShapeDtypeStruct((rows, levels, cells), populations.dtype), (2,) + half_side,
            like(emit_table), like(lines), like(places), like(walls), like(sources),
        ],
        *in_hbm(populations, absorb_table, emit_table, lines, places, walls, sources),
        space=HBM,
        scratch=[
            pltpu.VMEM(populations.shape, populations.dtype),
            pltpu.VMEM(absorb_table.shape, absorb_table.dtype),
            pltpu.SemaphoreType.DMA((13,)),
        ],
    )
    far_0 = lax.ppermute(mine_0, ("normal", "surf"), far[0])
    current, mine_1, *near_mine, select, weight = call(
        near_kernel,
        [
            whole, (2,) + half_side, (2,) + half_side, (2,) + half_side,
            jax.ShapeDtypeStruct((3, 2 * LANES, 4 * LANES), jnp.bfloat16), (3, 4, LANES),
        ],
        lines, kappa, places,
    )
    mine = (mine_0, mine_1)
    far_both = (far_0, lax.ppermute(mine_1, ("normal", "surf"), far[1]))
    near_both = [lax.ppermute(value, "surf", near) for value in near_mine]
    base, face, emission, rhs, own_couple = call(
        own_kernel, [whole, whole, whole, whole, (4,) + whole],
        kappa, current, turned, emit, sources, walls, select, weight,
    )
    firsts, others, meets = [], [], []
    for i in range(2):
        firsts.append(call(
            functools.partial(first_kernel, i * half),
            [(2, 4) + half_side, half_whole, half_whole, half_whole, (2 if i else 4, half, cells)],
            kappa, base, face, rhs, mine[i], far_both[i], near_mine[i], near_both[i], select, weight,
            *[done[4] for done in firsts],
            scratch=[found_both],
        ))
        others.append(lax.ppermute(firsts[i][4], "normal", swap))
    for i in range(2):
        couple, pivot, carried, solved, ends = firsts[i]
        meets.append(call(
            functools.partial(meet_kernel, 2 + i), [half_whole, half_side, half_side, (2, half, cells)],
            ends, others[i], firsts[0][4], others[0], carried, solved,
        ))
    far_current = [lax.ppermute(meets[i][1], ("normal", "surf"), far[2 + i]) for i in range(2)]
    near_current = [lax.ppermute(meet[2], "surf", near) for meet in meets]
    (rhs,) = call(own_again_kernel, [whole], meets[0][0], meets[1][0], emission, own_couple, select)
    parts = []
    for i in range(2):
        couple, pivot, carried, solved, ends = firsts[i]
        solved, end = call(
            functools.partial(again_kernel, i * half), [half_whole, (2, half, cells) if i else (half, cells)],
            rhs, far_current[i], near_current[i], couple, select, pivot, face, *parts[:1],
            scratch=[found_half],
        )
        parts += [end, meets[i][3], carried, solved]
    other_ends = lax.ppermute(end, "normal", swap)
    (out,) = call(
        last_kernel, [lines.shape], end, other_ends, *parts[1:4], *parts[5:],
        out_space=HBM,
        scratch=[pltpu.VMEM(lines.shape, jnp.float32), pltpu.SemaphoreType.DMA((4,))],
    )
    return out.reshape(groups, rows, cells)


def solution(mesh):
    return jax.shard_map(
        body,
        mesh=mesh,
        in_specs=(
            P(None, "normal", "surf"),
            P(),
            P(),
            P(None, "normal", "surf"),
            P(),
            P("surf", None),
            P("surf"),
        ),
        out_specs=P(None, "normal", "surf"),
        check_vma=False,
    )
```

```python
import functools

import jax
import jax.numpy as jnp
from jax import lax
from jax.experimental import pallas as pl
from jax.experimental.pallas import tpu as pltpu
from jax.sharding import PartitionSpec as P

HALO = 32
LANES = 128
HALF = 64
SURF_WEIGHT = 0.02
FACE = 2.0 / 3.0
LIMIT = 32 * 1024 * 1024
ACROSS = (False, True, False, False)


def inverse(value):
    guess = pl.reciprocal(value, approx=True)
    return guess * (2.0 - value * guess)


def lane_ids(rows):
    return lax.broadcasted_iota(jnp.int32, (rows, LANES), 1)


def gather(value, select):
    high = value.astype(jnp.bfloat16)
    low = (value - high.astype(jnp.float32)).astype(jnp.bfloat16)
    return jnp.dot(jnp.concatenate([high, low], axis=1), select, preferred_element_type=jnp.float32)


def selection(lanes):
    source = lax.broadcasted_iota(jnp.int32, (LANES, LANES), 0)
    parts = [jnp.where(source == lanes[s : s + 1], 1.0, 0.0).astype(jnp.bfloat16) for s in range(4)]
    one = jnp.concatenate(parts, axis=1)
    return jnp.concatenate([one, one], axis=0)


def cut(value, s):
    return value[:, s * LANES : (s + 1) * LANES]


def row_of(position, count):
    block = lax.axis_index("normal")
    return position + block * (count - 1 - 2 * position)


def odd_surf():
    return lax.rem(lax.axis_index("surf"), 2)


def pack(plane, high):
    size = plane.shape[0] // 4
    slot = lane_ids(size) // HALO
    packed = None
    for k in range(4):
        turned = pltpu.roll(plane[k * size : (k + 1) * size], HALO * lax.rem(k + high, 4), 1)
        packed = turned if k == 0 else jnp.where(slot == k, turned, packed)
    return packed


def local_places(neighbours_ref):
    offset = lax.axis_index("surf") * LANES
    found = neighbours_ref[...]
    return found >= 0, found - offset


def spread(table, rows):
    return [jnp.broadcast_to(table[s : s + 1], (rows, LANES)) for s in range(4)]


def own_tables(neighbours_ref):
    valid, local = local_places(neighbours_ref)
    inside = valid & (local >= 0) & (local < LANES)
    return jnp.where(inside, local, -1), jnp.where(inside, SURF_WEIGHT * FACE, 0.0)


def side_tables(neighbours_ref, high):
    valid, local = local_places(neighbours_ref)
    slot = lane_ids(4) // HALO
    place = local + (HALO - high * (LANES + HALO))
    here = slot == 3 * high
    beyond = valid & here & (place >= 0) & (place < HALO)
    place = jnp.where(beyond, place, -LANES)
    weight = jnp.where(beyond, SURF_WEIGHT * FACE, 0.0)

    def repeat(value):
        value = jnp.where(here, value, 0)
        return value + pltpu.roll(value, HALO, 1) + pltpu.roll(value, 2 * HALO, 1) + pltpu.roll(value, 3 * HALO, 1)

    return repeat(place) + HALO * slot, repeat(weight)


def unpack(value, high):
    here = lane_ids(value.shape[0]) // HALO == 3 * high
    return jnp.concatenate(
        [jnp.where(here, pltpu.roll(value, HALO * lax.rem(4 - k - high, 4), 1), 0.0) for k in range(4)], axis=0
    )


def kappa_kernel(pops_hbm, absorb_hbm, emit_hbm, lines_hbm, places_hbm, walls_hbm, sources_hbm, kappa_ref, turned_ref, far_0, emit_ref, lines_ref, places_ref, walls_ref, sources_ref, pops_ref, table_ref, sems):
    rows, groups, cells = kappa_ref.shape
    levels = pops_ref.shape[0]
    pieces = 4
    step = levels // pieces
    pairs = []
    for piece in range(pieces):
        here = pl.ds(piece * step, step)
        pairs.append((pops_hbm.at[here], pops_ref.at[here]))
    pairs.append((absorb_hbm, table_ref))
    step = groups * rows // pieces
    for piece in range(pieces):
        there = pl.ds(piece * step, step)
        pairs.append((lines_hbm.at[there], lines_ref.at[there]))
    pairs += [(emit_hbm, emit_ref), (places_hbm, places_ref), (walls_hbm, walls_ref), (sources_hbm, sources_ref)]
    copies = [pltpu.make_async_copy(pair[0], pair[1], sems.at[i]) for i, pair in enumerate(pairs)]
    for copy in copies:
        copy.start()
    step = levels // pieces
    for piece in range(pieces):
        copies[piece].wait()
        here = pl.ds(piece * step, step)
        turned_ref[:, here, :] = jnp.swapaxes(pops_ref[here], 0, 1)
    copies[pieces].wait()
    table = table_ref[...]
    for pair in range(rows // 2):
        both = jnp.concatenate([turned_ref[2 * pair], turned_ref[2 * pair + 1]], axis=1)
        product = jnp.dot(table, both, preferred_element_type=jnp.float32)
        for k in range(2):
            kappa_ref[row_of(2 * pair + k, rows)] = product[:, k * cells : (k + 1) * cells]
    odd = odd_surf()
    half = groups // 2
    for r in range(rows):
        far_0[0, r] = pack(kappa_ref[r, :half], odd)
    for copy in copies[pieces + 1 :]:
        copy.wait()
    for r in range(rows):
        far_0[1, r] = pack(lines_ref[pl.ds(row_of(r, rows), half, stride=rows), :], odd)


def near_kernel(lines_ref, kappa_ref, neighbours_ref, current_ref, far_1, near_0, near_1, select_ref, weight_ref):
    rows, groups, cells = current_ref.shape
    half = groups // 2
    high = odd_surf()
    low_near = 1 - high
    for r in range(rows):
        current = lines_ref[pl.ds(row_of(r, rows), groups, stride=rows), :]
        current_ref[r] = current
        kappa = kappa_ref[r]
        far_1[0, r] = pack(kappa[half:], high)
        far_1[1, r] = pack(current[half:], high)
        near_0[0, r] = pack(kappa[:half], low_near)
        near_0[1, r] = pack(current[:half], low_near)
        near_1[0, r] = pack(kappa[half:], low_near)
        near_1[1, r] = pack(current[half:], low_near)
    lanes, weight = own_tables(neighbours_ref)
    select_ref[0] = selection(lanes)
    weight_ref[0] = weight
    lanes, weight = side_tables(neighbours_ref, low_near)
    select_ref[1] = selection(lanes)
    weight_ref[1] = weight
    lanes, weight = side_tables(neighbours_ref, high)
    select_ref[2] = selection(lanes)
    weight_ref[2] = weight


def own_kernel(kappa_ref, current_ref, turned_ref, emit_ref, source_ref, wall_ref, select_ref, weight_ref, base_ref, face_ref, emission_ref, rhs_ref, couple_ref):
    rows, groups, cells = kappa_ref.shape
    weight = spread(weight_ref[0], groups)
    kind = wall_ref[...]
    share = jnp.where(kind == 0, 0.5, jnp.where(kind == 1, 0.25, 0.0))
    at_wall = lax.axis_index("normal") == 0
    boundary = jnp.where(at_wall, share, 0.5)
    source = jnp.broadcast_to(source_ref[...], (groups, groups)).T * jnp.where(at_wall, share, 0.0)
    table = emit_ref[...]
    for pair in range(rows // 2):
        both = jnp.concatenate([turned_ref[2 * pair], turned_ref[2 * pair + 1]], axis=1)
        product = jnp.dot(table, both, preferred_element_type=jnp.float32)
        for k in range(2):
            emission_ref[row_of(2 * pair + k, rows)] = product[:, k * cells : (k + 1) * cells]
    emission_ref[0] = emission_ref[0] + source

    @pl.loop(0, rows // 4)
    def _(quad):
        here = pl.ds(quad * 4, 4)
        planes = jnp.concatenate([kappa_ref[here], current_ref[here]], axis=0).reshape(8 * groups, cells)
        found = gather(planes, select_ref[0])
        for k in range(4):
            r = quad * 4 + k
            kappa = kappa_ref[r]
            total = kappa + jnp.where(r == 0, boundary, 0.0) if k == 0 else kappa
            rhs = emission_ref[r]
            for s in range(4):
                couple = weight[s] * inverse(kappa + cut(found[k * groups : (k + 1) * groups], s))
                couple_ref[s, r] = couple
                total = total + couple
                rhs = rhs + couple * cut(found[(4 + k) * groups : (5 + k) * groups], s)
            base_ref[r] = total
            rhs_ref[r] = rhs
            face_ref[r] = FACE * inverse(kappa_ref[jnp.maximum(r - 1, 0)] + kappa)


def own_again_kernel(current_0, current_1, emission_ref, couple_ref, select_ref, rhs_ref):
    rows, groups, cells = emission_ref.shape

    @pl.loop(0, rows // 4)
    def _(quad):
        here = pl.ds(quad * 4, 4)
        planes = jnp.concatenate([current_0[here], current_1[here]], axis=1).reshape(4 * groups, cells)
        found = gather(planes, select_ref[0])
        for k in range(4):
            r = quad * 4 + k
            rhs = emission_ref[r]
            for s in range(4):
                rhs = rhs + couple_ref[s, r] * cut(found[k * groups : (k + 1) * groups], s)
            rhs_ref[r] = rhs


def find_sides(far, near, select_ref, found_ref):
    found_ref[0] = gather(far, select_ref[2]).reshape(found_ref.shape[1:])
    found_ref[1] = gather(near, select_ref[1]).reshape(found_ref.shape[1:])


def first_kernel(start, kappa_ref, base_ref, face_ref, rhs_ref, mine_ref, far_ref, near_mine_ref, near_ref, select_ref, weight_ref, *refs):
    couple_ref, pivot_ref, carried_ref, solved_ref, ends_ref, found_ref = refs[-6:]
    rows, groups, cells = pivot_ref.shape
    size = groups // 4
    here = pl.ds(start, groups)
    if start == 0:
        ends_ref[2] = kappa_ref[rows - 1, here]
        ends_ref[3] = kappa_ref[rows - 1, pl.ds(groups, groups)]
    high = odd_surf()
    find_sides(far_ref[...].reshape(2 * rows * size, cells), near_ref[...].reshape(2 * rows * size, cells), select_ref, found_ref)
    weights = [spread(weight_ref[2], size), spread(weight_ref[1], size)]
    schur = None
    carried = None
    solved = None
    for r in range(rows):
        base = base_ref[r, here, :]
        rhs = rhs_ref[r, here, :]
        for side in range(2):
            kappa = (near_mine_ref if side else mine_ref)[0, r]
            for s in range(4):
                couple = weights[side][s] * inverse(kappa + cut(found_ref[side, r], s))
                couple_ref[side, s, r] = couple
                term = couple * cut(found_ref[side, rows + r], s)
                total = couple if s == 0 else total + couple
                terms = term if s == 0 else terms + term
            base = base + unpack(total, 1 - high if side else high)
            rhs = rhs + unpack(terms, 1 - high if side else high)
        if r == 0:
            schur = base
        else:
            schur = base + schur * carried
            rhs = rhs + face_ref[r, here, :] * solved
        if r == rows - 1:
            ends_ref[0] = schur
            ends_ref[1] = rhs
        else:
            after = face_ref[r + 1, here, :]
            pivot = inverse(schur + after)
            carried = after * pivot
            solved = rhs * pivot
            pivot_ref[r] = pivot
            carried_ref[r] = carried
            solved_ref[r] = solved


def meet_kernel(edge, ends_ref, other_ref, edges_ref, other_edges_ref, carried_ref, solved_ref, current_ref, far_ref, near_ref, mix_ref):
    rows, groups, cells = current_ref.shape
    odd = odd_surf()
    face = FACE * inverse(edges_ref[edge] + other_edges_ref[edge])
    own, other = ends_ref[0], other_ref[0]
    scale = inverse(own * other + face * (own + other))
    mine = (other + face) * scale
    theirs = face * scale
    mix_ref[0] = mine
    mix_ref[1] = theirs
    value = mine * ends_ref[1] + theirs * other_ref[1]
    current_ref[rows - 1] = value
    far_ref[rows - 1] = pack(value, odd)
    near_ref[rows - 1] = pack(value, 1 - odd)
    for r in range(rows - 2, -1, -1):
        value = solved_ref[r] + carried_ref[r] * value
        current_ref[r] = value
        far_ref[r] = pack(value, odd)
        near_ref[r] = pack(value, 1 - odd)


def again_kernel(start, rhs_ref, far_ref, near_ref, couple_ref, select_ref, pivot_ref, face_ref, *refs):
    solved_ref, end_ref, found_ref = refs[-3:]
    if len(refs) > 3:
        end_ref[0] = refs[0][...]
        end_ref = end_ref.at[1]
    rows, groups, cells = pivot_ref.shape
    size = groups // 4
    here = pl.ds(start, groups)
    high = odd_surf()
    find_sides(far_ref[...].reshape(rows * size, cells), near_ref[...].reshape(rows * size, cells), select_ref, found_ref)
    solved = None
    for r in range(rows):
        rhs = rhs_ref[r, here, :]
        for side in range(2):
            for s in range(4):
                term = couple_ref[side, s, r] * cut(found_ref[side, r], s)
                terms = term if s == 0 else terms + term
            rhs = rhs + unpack(terms, 1 - high if side else high)
        if r > 0:
            rhs = rhs + face_ref[r, here, :] * solved
        if r == rows - 1:
            end_ref[...] = rhs
        else:
            solved = rhs * pivot_ref[r]
            solved_ref[r] = solved


def last_kernel(*refs):
    ends_ref, others_ref, *halves, out_hbm, lines_ref, sems = refs
    copies = []
    start = 0
    for i in range(2):
        mix_ref, carried_ref, solved_ref = halves[3 * i : 3 * i + 3]
        end_ref, other_ref = ends_ref.at[i], others_ref.at[i]
        rows, groups, cells = carried_ref.shape
        step = groups // 4
        for part in range(4):
            here = pl.ds(part * step, step)
            value = mix_ref[0, here, :] * end_ref[here, :] + mix_ref[1, here, :] * other_ref[here, :]
            lines_ref[pl.ds(start * rows + row_of(rows - 1, rows), step, stride=rows), :] = value
            for r in range(rows - 2, -1, -1):
                value = solved_ref[r, here, :] + carried_ref[r, here, :] * value
                lines_ref[pl.ds(start * rows + row_of(r, rows), step, stride=rows), :] = value
            there = pl.ds(start * rows, step * rows)
            copies.append(pltpu.make_async_copy(lines_ref.at[there], out_hbm.at[there], sems.at[len(copies)]))
            copies[-1].start()
            start = start + step
    for copy in copies:
        copy.wait()


VMEM = pl.BlockSpec(memory_space=pltpu.VMEM)
HBM = pl.BlockSpec(memory_space=pltpu.HBM)


def call(kernel, outs, *args, space=VMEM, out_space=VMEM, scratch=()):
    return pl.pallas_call(
        kernel,
        out_shape=[jax.ShapeDtypeStruct(out, jnp.float32) if isinstance(out, tuple) else out for out in outs],
        in_specs=[space] * len(args),
        out_specs=[out_space] * len(outs),
        scratch_shapes=list(scratch),
        compiler_params=pltpu.CompilerParams(vmem_limit_bytes=LIMIT),
    )(*args)


def like(value):
    return jax.ShapeDtypeStruct(value.shape, value.dtype)


def in_hbm(*values):
    return [pltpu.with_memory_space_constraint(value, pltpu.HBM) for value in values]


def far_pairs(count, across):
    pairs = []
    for block in range(2):
        for i in range(count):
            if i in (0, count - 1):
                other = count - 1 - i if across else i
                pairs.append((block * count + i, (1 - block) * count + other))
            else:
                pairs.append((block * count + i, block * count + (i + 1 if i % 2 else i - 1)))
    return pairs


def body(populations, absorb_table, emit_table, energy, wall_source, neighbours, wall_type):
    levels, rows, cells = populations.shape
    groups = absorb_table.shape[0]
    whole = (rows, groups, cells)
    plane = (groups, cells)
    side = (rows, HALO, cells)
    half = groups // 2
    half_whole = (rows, half, cells)
    half_side = (rows, HALO // 2, cells)
    found_half = pltpu.VMEM((2, rows, HALO // 2, 4 * LANES), jnp.float32)
    found_both = pltpu.VMEM((2, 2 * rows, HALO // 2, 4 * LANES), jnp.float32)
    count = lax.axis_size("surf")
    far = [far_pairs(count, across) for across in ACROSS]
    near = [(i, i ^ 1) for i in range(count)]
    swap = [(0, 1), (1, 0)]
    lines = energy.reshape(groups * rows, cells)
    places = neighbours.T
    walls = wall_type.reshape(1, cells)
    sources = wall_source.reshape(1, groups)

    kappa, turned, mine_0, emit, lines, places, walls, sources = call(
        kappa_kernel,
        [
            whole, jax.ShapeDtypeStruct((rows, levels, cells), populations.dtype), (2,) + half_side,
            like(emit_table), like(lines), like(places), like(walls), like(sources),
        ],
        *in_hbm(populations, absorb_table, emit_table, lines, places, walls, sources),
        space=HBM,
        scratch=[
            pltpu.VMEM(populations.shape, populations.dtype),
            pltpu.VMEM(absorb_table.shape, absorb_table.dtype),
            pltpu.SemaphoreType.DMA((13,)),
        ],
    )
    far_0 = lax.ppermute(mine_0, ("normal", "surf"), far[0])
    current, mine_1, *near_mine, select, weight = call(
        near_kernel,
        [
            whole, (2,) + half_side, (2,) + half_side, (2,) + half_side,
            jax.ShapeDtypeStruct((3, 2 * LANES, 4 * LANES), jnp.bfloat16), (3, 4, LANES),
        ],
        lines, kappa, places,
    )
    mine = (mine_0, mine_1)
    far_both = (far_0, lax.ppermute(mine_1, ("normal", "surf"), far[1]))
    near_both = [lax.ppermute(value, "surf", near) for value in near_mine]
    base, face, emission, rhs, own_couple = call(
        own_kernel, [whole, whole, whole, whole, (4,) + whole],
        kappa, current, turned, emit, sources, walls, select, weight,
    )
    firsts, others, meets = [], [], []
    for i in range(2):
        firsts.append(call(
            functools.partial(first_kernel, i * half),
            [(2, 4) + half_side, half_whole, half_whole, half_whole, (2 if i else 4, half, cells)],
            kappa, base, face, rhs, mine[i], far_both[i], near_mine[i], near_both[i], select, weight,
            *[done[4] for done in firsts],
            scratch=[found_both],
        ))
        others.append(lax.ppermute(firsts[i][4], "normal", swap))
    for i in range(2):
        couple, pivot, carried, solved, ends = firsts[i]
        meets.append(call(
            functools.partial(meet_kernel, 2 + i), [half_whole, half_side, half_side, (2, half, cells)],
            ends, others[i], firsts[0][4], others[0], carried, solved,
        ))
    far_current = [lax.ppermute(meets[i][1], ("normal", "surf"), far[2 + i]) for i in range(2)]
    near_current = [lax.ppermute(meet[2], "surf", near) for meet in meets]
    (rhs,) = call(own_again_kernel, [whole], meets[0][0], meets[1][0], emission, own_couple, select)
    parts = []
    for i in range(2):
        couple, pivot, carried, solved, ends = firsts[i]
        solved, end = call(
            functools.partial(again_kernel, i * half), [half_whole, (2, half, cells) if i else (half, cells)],
            rhs, far_current[i], near_current[i], couple, select, pivot, face, *parts[:1],
            scratch=[found_half],
        )
        parts += [end, meets[i][3], carried, solved]
    other_ends = lax.ppermute(end, "normal", swap)
    (out,) = call(
        last_kernel, [lines.shape], end, other_ends, *parts[1:4], *parts[5:],
        out_space=HBM,
        scratch=[pltpu.VMEM(lines.shape, jnp.float32), pltpu.SemaphoreType.DMA((8,))],
    )
    return out.reshape(groups, rows, cells)


def solution(mesh):
    return jax.shard_map(
        body,
        mesh=mesh,
        in_specs=(
            P(None, "normal", "surf"),
            P(),
            P(),
            P(None, "normal", "surf"),
            P(),
            P("surf", None),
            P("surf"),
        ),
        out_specs=P(None, "normal", "surf"),
        check_vma=False,
    )
```
